128 devices in a mesh: dp: 32 (over z, y, core), tensor: 4 (over x).
Axes of the slice: x: 4, y: 4, z: 4, core: 2. Of those that a mesh axis runs over, the one named last changes fastest.
Arguments:
- tokens: bfloat16 [16384, 768], P('dp'), may hold values from -6 to 6
- cotangent: bfloat16 [16384, 768], P('dp'), may hold values from -6 to 6
- buckets: int32 [256], P('dp'), may hold values from 0 to 1999
- time_table: bfloat16 [2000, 768], replicated, may hold values from -6 to 6
- w_qkv: bfloat16 [2, 768, 3, 768], P(None, None, None, 'tensor'), may hold values from -0.21875 to 0.21875
- w_out: bfloat16 [2, 768, 768], P(None, 'tensor'), may hold values from -1.75 to 1.75
- w_up: bfloat16 [2, 768, 3072], P(None, None, 'tensor'), may hold values from -0.21875 to 0.21875
- w_down: bfloat16 [2, 3072, 768], P(None, 'tensor'), may hold values from -0.15625 to 0.15625
- norm_gain: float32 [2, 2, 768], replicated, may hold values from 0.5 to 1.5
- norm_bias: float32 [2, 2, 768], replicated, may hold values from -3 to 3
Outputs:
- layer_out: bfloat16 [16384, 768], P('dp')
- token_grad: float32 [16384, 768], P('dp')
- table_grad: float32 [2000, 768], P(None, 'tensor')
- qkv_grad: float32 [2, 768, 3, 768], P(None, None, None, 'tensor')
- out_grad: float32 [2, 768, 768], P(None, 'tensor')
- up_grad: float32 [2, 768, 3072], P(None, None, 'tensor')
- down_grad: float32 [2, 3072, 768], P(None, 'tensor')
- gain_grad: float32 [2, 2, 768], replicated
- bias_grad: float32 [2, 2, 768], replicated
The draws below stay inside these ranges and needn't reach their ends.
All inputs are finite; a program needn't handle non-finite values.
Results may differ from the reference program's by a relative error of at most 0.01.
Values sent between devices are 32-bit elements; how exact they have to be, the bound alone decides.
A program may use at most 128 MiB of HBM per device.

```python
import math
import jax
import jax.numpy as jnp
import numpy as np
from jax import lax

D = 768
HEADS = 12
HEAD_DIM = 64
FF = 3072
BUCKETS = 2000
LAYERS = 2
SEQ_LEN = 64
SEQ_DEV = 8
SENTENCES = 256
TOKENS = 16384
N_DP = 32


def with_ends(drawn, own_key, low, largest):
    spot = [jax.random.randint(jax.random.fold_in(own_key, axis), (), 0, length) for axis, length in enumerate(drawn.shape)]
    main_axis = drawn.shape.index(max(drawn.shape))
    beside = spot[:main_axis] + [(spot[main_axis] + 1) % drawn.shape[main_axis]] + spot[main_axis + 1:]
    return drawn.at[tuple(spot)].set(low).at[tuple(beside)].set(largest)


def block_levels(rng, dims, shards, smallest, top_value):
    loudness = 1.0
    for axis_at, shards_of in shards:
        steps = jax.random.uniform(jax.random.fold_in(jax.random.fold_in(rng, 6), axis_at), (shards_of,), jnp.float32, smallest / len(shards), top_value / len(shards))
        loudness = loudness * jnp.repeat(jnp.exp(steps), dims[axis_at] // shards_of).reshape((-1,) + (1,) * (len(dims) - 1 - axis_at))
    return loudness


def rank_table(number_of, slope):
    weights = [(1 << 20) // math.isqrt(rank ** slope) + 1 for rank in range(1, number_of + 1)]
    spread = 1 + sum(weights) // (1 << 30)
    return np.cumsum(np.array([max(1, weight // spread) for weight in weights]))


def ranked_ids(rng, shape, amount, skew):
    grid = rank_table(amount, skew)
    ticket = jax.random.randint(jax.random.fold_in(rng, 1), shape, 0, int(grid[amount - 1]))
    rank = jnp.searchsorted(jnp.asarray(grid, jnp.int32), ticket, side="right")
    return jax.random.permutation(jax.random.fold_in(rng, 2), amount)[rank].astype(jnp.int32)


def scatter_about(key, dims, spread, reach, split=(), dtype=jnp.bfloat16):
    drawn = jax.random.normal(key, dims, jnp.float32) * spread
    if len(split) > 0:
        drawn = block_levels(key, dims, split, -0.22, 0.18) * drawn
    return jnp.clip(drawn, min=-reach, max=reach).astype(dtype)


def setup_inputs(seed: int = 0) -> dict:
    key_of = jax.random.split(jax.random.key(seed), 11)
    return {
        "tokens": scatter_about(key_of[0], (TOKENS, D), 1.0, 6.0, ((0, 32),)),
        "cotangent": scatter_about(key_of[1], (TOKENS, D), 1.0, 6.0, ((0, 32),)),
        "buckets": with_ends(ranked_ids(key_of[2], (SENTENCES,), BUCKETS, 2), jax.random.fold_in(key_of[2], 3), 0, BUCKETS - 1).astype(jnp.int32),
        "time_table": scatter_about(key_of[3], (BUCKETS, D), 1.0, 6.0),
        "w_qkv": scatter_about(key_of[4], (LAYERS, D, 3, D), D ** -0.5, 0.21875, ((3, 4),)),
        "w_out": scatter_about(key_of[5], (LAYERS, D, D), (D // SEQ_LEN) ** -0.5, 1.75, ((1, 4),)),
        "w_up": scatter_about(key_of[6], (LAYERS, D, FF), D ** -0.5, 0.21875, ((2, 4),)),
        "w_down": scatter_about(key_of[7], (LAYERS, FF, D), (FF // 2) ** -0.5, 0.15625, ((1, 4),)),
        "norm_gain": jnp.clip(1.0 + 0.1 * jax.random.normal(key_of[8], (LAYERS, 2, D), jnp.float32), 0.5, 1.5),
        "norm_bias": scatter_about(key_of[9], (LAYERS, 2, D), 0.5, 3.0, (), jnp.float32),
    }


@jax.custom_vjp
def low(v):
    return lax.optimization_barrier(v.astype(jnp.bfloat16)).astype(jnp.float32)

@jax.custom_vjp
def low_back(v):
    return v

def low_keep(v):
    return (low(v), None)

def low_pass(kept, grad):
    return (grad,)

def back_keep(v):
    return (v, None)

def back_low(kept, grad):
    return (low(grad),)
low.defvjp(low_keep, low_pass)
low_back.defvjp(back_keep, back_low)
norm_eps = 1e-05
highest = lax.Precision.HIGHEST

def layer_norm(x, weight_row, shift_row):
    row_mean = lax.optimization_barrier(jnp.mean(x, axis=-1, keepdims=True))
    centred = x - row_mean
    row_var = lax.optimization_barrier(jnp.mean(centred * centred, axis=-1, keepdims=True))
    return centred * lax.rsqrt(row_var + norm_eps) * weight_row + shift_row

def one_layer(x, wqkv, wout, wup, wdown, gains, shifts, sentence_count):
    row_count = x.shape[0]
    normed = low(layer_norm(x, gains[0], shifts[0]))
    qkv_all = low(low_back(jnp.einsum('rd,dcf->rcf', normed, wqkv, precision=highest)))
    qkv_heads = qkv_all.reshape(sentence_count, SEQ_LEN, 3, HEADS, HEAD_DIM)
    scores = jnp.einsum('sqhe,skhe->shqk', qkv_heads[:, :, 0], qkv_heads[:, :, 1], precision=highest)
    scores = low_back(scores * HEAD_DIM ** (-0.5))
    attn_probs = low(jax.nn.softmax(scores, axis=-1))
    head_mix = jnp.einsum('shqk,skhe->sqhe', attn_probs, qkv_heads[:, :, 2], precision=highest)
    head_mix = low(low_back(head_mix.reshape(row_count, D)))
    hidden = x + low_back(jnp.dot(head_mix, wout, precision=highest))
    normed_two = low(layer_norm(hidden, gains[1], shifts[1]))
    upward = low_back(jnp.dot(normed_two, wup, precision=highest))
    active = low(jax.nn.gelu(upward))
    return hidden + low_back(jnp.dot(active, wdown, precision=highest))

def reference(tokens, cotangent, buckets, time_table, w_qkv, w_out, w_up, w_down, norm_gain, norm_bias):
    weights = (time_table.astype(jnp.float32), w_qkv.astype(jnp.float32), w_out.astype(jnp.float32), w_up.astype(jnp.float32), w_down.astype(jnp.float32), norm_gain, norm_bias)
    tok_blocks = tokens.reshape(N_DP, SEQ_DEV * SEQ_LEN, D)
    cot_blocks = cotangent.reshape(N_DP, SEQ_DEV * SEQ_LEN, D)
    bucket_blocks = buckets.reshape(N_DP, SEQ_DEV)

    def step(carry, block):
        tok_rows, cot_rows, bucket_rows = block

        def forward(x_tok, table, wqkv, wout, wup, wdown, gains, shifts):
            x = x_tok + jnp.repeat(table[bucket_rows], SEQ_LEN, axis=0)
            for layer_idx in range(LAYERS):
                x = one_layer(x, wqkv[layer_idx], wout[layer_idx], wup[layer_idx], wdown[layer_idx], gains[layer_idx], shifts[layer_idx], SEQ_DEV)
            return x
        result, pullback = jax.vjp(forward, tok_rows.astype(jnp.float32), *weights)
        grads = pullback(cot_rows.astype(jnp.float32))
        carry = jax.tree.map(lambda a, b: a + b, carry, tuple(grads[1:]))
        return (carry, (result.astype(jnp.bfloat16), grads[0]))
    zeros = tuple((jnp.zeros(w.shape, jnp.float32) for w in weights))
    totals, (outputs, tok_grads) = lax.scan(step, zeros, (tok_blocks, cot_blocks, bucket_blocks))
    return (outputs.reshape(TOKENS, D), tok_grads.reshape(TOKENS, D), totals[0], totals[1], totals[2], totals[3], totals[4], totals[5], totals[6])
```

```python
import functools

import jax
import jax.numpy as jnp
from jax import lax
from jax.experimental import pallas as pl
from jax.experimental.pallas import tpu as pltpu
from jax.sharding import PartitionSpec as P

MESH = pl.DeviceIdType.MESH
F32 = jnp.float32
BF16 = jnp.bfloat16
HEAD_DIM = 64
SEQ_LEN = 64
D = 768
ROWS = 512
BLK = 128
HALF = 64
COLS = 256
EPS = 1e-05
GELU_A = 0.7978845608028654
GELU_B = 0.044715


def nn(a, b):
    return lax.dot_general(a, b, (((1,), (0,)), ((), ())), preferred_element_type=F32)


def nt(a, b):
    return lax.dot_general(a, b, (((1,), (1,)), ((), ())), preferred_element_type=F32)


def tn(a, b):
    return lax.dot_general(a, b, (((0,), (0,)), ((), ())), preferred_element_type=F32)


def norm_parts(x):
    c = x - jnp.mean(x, axis=-1, keepdims=True)
    r = lax.rsqrt(jnp.mean(c * c, axis=-1, keepdims=True) + EPS)
    return c * r, r


def norm(x, g, b):
    return norm_parts(x)[0] * g + b


def norm_back(dn, x, g):
    xh, r = norm_parts(x)
    dx = dn * g
    dx = r * (dx - jnp.mean(dx, axis=-1, keepdims=True) - xh * jnp.mean(dx * xh, axis=-1, keepdims=True))
    return dx, jnp.sum(dn * xh, axis=0, keepdims=True), jnp.sum(dn, axis=0, keepdims=True)


def gelu_cdf(u):
    t = jnp.tanh(GELU_A * (u + GELU_B * (u * u * u)))
    return t, 0.5 + 0.5 * t


def gelu(u):
    return u * gelu_cdf(u)[1]


def gelu_slope(u):
    t, cdf = gelu_cdf(u)
    return cdf + u * (0.5 * (1.0 - t * t)) * (GELU_A * (1.0 + 3.0 * GELU_B * (u * u)))


def body(nz, ny, nx,
         tok_ref, trow_ref, cot_ref, wqkv_ref, wout_ref, wup_ref, wdown_ref, gain_ref, bias_ref,
         lo_ref, tg_ref, gm1_ref, ga1_ref, gm0_ref, ga0_ref, vec_ref,
         ag, sbuf, rh, rf, n1, n2, act, q, k, v, o, u, prob, hs, xs, carry, low, du, dq, dk, dv,
         rs_s, rs_r, ag_s, ag_r):
    dp = lax.axis_index("dp")
    me = lax.axis_index("tensor")
    right = (dp, lax.rem(me + 1, nx))
    left = (dp, lax.rem(me + nx - 1, nx))
    across = (dp, lax.rem(me + 2, nx))

    bar = pltpu.get_barrier_semaphore()
    peers = [right, left]
    for peer in peers:
        pl.semaphore_signal(bar, inc=1, device_id=peer, device_id_type=MESH)
    pl.semaphore_wait(bar, len(peers))

    def rows(b):
        return pl.ds(pl.multiple_of(b * BLK, BLK), BLK)

    def half(b, i):
        return pl.ds(pl.multiple_of(b * BLK + i * HALF, HALF), HALF)

    def turn(rel):
        return lax.rem(me + rel, nx)

    mine = rows(me)

    def rs_copy(i):
        src, dst, to = [
            (sbuf.at[0, 0:HALF], rh.at[0], right),
            (sbuf.at[0, HALF:BLK], rh.at[1], left),
            (sbuf.at[1, HALF:BLK], rf.at[0, HALF:BLK], right),
            (sbuf.at[2, 0:HALF], rf.at[1, 0:HALF], left),
            (sbuf.at[1, 0:HALF], rf.at[0, 0:HALF], right),
            (sbuf.at[2, HALF:BLK], rf.at[1, HALF:BLK], left),
        ][i]
        return pltpu.make_async_remote_copy(
            src_ref=src, dst_ref=dst, send_sem=rs_s.at[i], recv_sem=rs_r.at[i], device_id=to, device_id_type=MESH)

    def rs_send(part):
        def step(j, _):
            blk = turn(jnp.where(j == 0, 2, jnp.where(j == 1, 1, jnp.where(j == 2, 3, 0))))
            for c in range(D // COLS):
                sbuf[j, :, c * COLS:(c + 1) * COLS] = part(rows(blk), c)

            @pl.when(j == 0)
            def _():
                rs_copy(0).start()
                rs_copy(1).start()

            @pl.when(j == 1)
            def _():
                rs_copy(2).start()

            @pl.when(j == 2)
            def _():
                rs_copy(3).start()
                rs_copy(0).wait_recv()
                sbuf[1, 0:HALF] += rh[0]
                rs_copy(4).start()
                rs_copy(1).wait_recv()
                sbuf[2, HALF:BLK] += rh[1]
                rs_copy(5).start()
            return 0
        lax.fori_loop(0, nx, step, 0)

    def rs_done():
        for i in range(2, 6):
            rs_copy(i).wait_recv()
        total = sbuf[3] + rf[0] + rf[1]
        for i in range(6):
            rs_copy(i).wait_send()
        return total

    def ag_copy(i, arriving=False):
        if arriving:
            b, h = [(3, 0), (1, 1), (3, 1), (1, 0), (2, 0), (2, 1)][i]
        else:
            b, h = [(0, 0), (0, 1), (0, 1), (0, 0), (3, 0), (1, 1)][i]
        at = half(turn(b), h)
        return pltpu.make_async_remote_copy(
            src_ref=ag.at[at], dst_ref=ag.at[at], send_sem=ag_s.at[i], recv_sem=ag_r.at[i],
            device_id=[right, left][i % 2], device_id_type=MESH)

    def ag_send(val):
        ag[mine] = val
        for i in range(4):
            ag_copy(i).start()

    def ag_take(fn):
        def step(j, _):
            blk = turn(jnp.where(j == 0, 0, jnp.where(j == 1, 3, jnp.where(j == 2, 1, 2))))

            @pl.when(j == 1)
            def _():
                ag_copy(0, True).wait_recv()
                ag_copy(4).start()
                ag_copy(1, True).wait_recv()
                ag_copy(5).start()
                ag_copy(2, True).wait_recv()

            @pl.when(j == 2)
            def _():
                ag_copy(3, True).wait_recv()

            @pl.when(j == 3)
            def _():
                ag_copy(4, True).wait_recv()
                ag_copy(5, True).wait_recv()
            fn(blk, rows(blk))
            return 0
        lax.fori_loop(0, nx, step, 0)
        for i in range(6):
            ag_copy(i).wait_send()

    def each(fn):
        def step(j, _):
            fn(j, rows(j))
            return 0
        lax.fori_loop(0, nx, step, 0)

    def g_of(l, i):
        return gain_ref[2 * l + i:2 * l + i + 1, :]

    def b_of(l, i):
        return bias_ref[2 * l + i:2 * l + i + 1, :]

    def x0(b, r):
        x = tok_ref[r].astype(F32)
        s = lax.broadcasted_iota(jnp.int32, (BLK, 1), 0) < SEQ_LEN
        return x + jnp.where(s, trow_ref[2 * b], trow_ref[2 * b + 1])

    iq = lax.broadcasted_iota(jnp.int32, (BLK, BLK), 0) // SEQ_LEN
    ik = lax.broadcasted_iota(jnp.int32, (BLK, BLK), 1) // SEQ_LEN
    same = iq == ik
    lane = lax.broadcasted_iota(jnp.int32, (1, BLK), 1) // HEAD_DIM
    heads = [(slice(0, 128), (lane == 0).astype(F32).astype(BF16)), (slice(0, 128), (lane == 1).astype(F32).astype(BF16)),
             (slice(128, 192), None)]

    def only(x, m):
        return x if m is None else x * m

    def attn_out(l, b, r):
        outs = []
        for i, (c, m) in enumerate(heads):
            s = nt(only(q[l, r, c], m), k[l, r, c]) * HEAD_DIM ** -0.5
            s = jnp.where(same, s, -1e30)
            e = jnp.exp(s - jnp.max(s, axis=-1, keepdims=True))
            p = e / jnp.sum(e, axis=-1, keepdims=True)
            prob[l, 3 * b + i] = p
            outs.append(nn(p.astype(BF16), only(v[l, r, c], m)))
        o[l, r, 0:128] = (outs[0] + outs[1]).astype(BF16)
        o[l, r, 128:192] = outs[2].astype(BF16)

    def qkv_attn(l, b, r, n):
        n1[l, r] = n
        for i, t in enumerate((q, k, v)):
            t[l, r, :] = nt(n, wqkv_ref[l, 192 * i:192 * (i + 1), :]).astype(BF16)
        attn_out(l, b, r)

    def attn_back(l, b, r, do):
        got = []
        for i, (c, m) in enumerate(heads):
            p = prob[l, 3 * b + i]
            pb = p.astype(BF16)
            d = only(do[:, c], m)
            dp_ = nt(d, v[l, r, c])
            ds = (p * (dp_ - jnp.sum(p * dp_, axis=-1, keepdims=True))).astype(BF16)
            got.append((nn(ds, only(k[l, r, c], m)), tn(ds, only(q[l, r, c], m)), tn(pb, d)))
        for t, j, s in ((dq, 0, HEAD_DIM ** -0.5), (dk, 1, HEAD_DIM ** -0.5), (dv, 2, 1.0)):
            t[r, 0:128] = ((got[0][j] + got[1][j]) * s).astype(BF16)
            t[r, 128:192] = (got[2][j] * s).astype(BF16)

    def mlp_up(l, r, n):
        n2[l, r] = n
        for c in range(D // COLS):
            cs = slice(c * COLS, (c + 1) * COLS)
            up = nn(n, wup_ref[l, :, cs])
            u[l, r, cs] = up
            act[l, r, cs] = gelu(up).astype(BF16)

    def mlp_back(l, r, gl):
        for c in range(D // COLS):
            cs = slice(c * COLS, (c + 1) * COLS)
            da = nt(gl, wdown_ref[l, cs, :])
            du[r, cs] = (da * gelu_slope(u[l, r, cs])).astype(BF16)

    def weight_grad(a, b, out, wide, at=0):
        for m in range(0, wide, 192):
            for c in range(D // COLS):
                cs = slice(c * COLS, (c + 1) * COLS)
                out[at + m:at + m + 192, cs] = tn(a[:, m:m + 192], b[:, cs])

    def weight_grad_wide(a, b, out):
        def step(i, _):
            at = pl.ds(pl.multiple_of(i * COLS, COLS), COLS)
            for c in range(D // COLS):
                cs = slice(c * COLS, (c + 1) * COLS)
                out[at, cs] = tn(a[:, at], b[:, cs])
            return 0
        lax.fori_loop(0, D // COLS, step, 0)

    def cols(c):
        return slice(c * COLS, (c + 1) * COLS)

    def vec_add(l, i, gg, bg):
        vec_ref[2 * l + i:2 * l + i + 1, :] = gg
        vec_ref[4 + 2 * l + i:5 + 2 * l + i, :] = bg

    def first(b, r):
        qkv_attn(0, b, r, norm(x0(b, r), g_of(0, 0), b_of(0, 0)).astype(BF16))
    each(first)
    x_own = x0(me, mine)
    for l in range(2):
        if l == 1:
            def attn_block(b, r):
                qkv_attn(1, b, r, ag[r].astype(BF16))
            ag_take(attn_block)
        rs_send(lambda r, c, l=l: nn(o[l, r], wout_ref[l, :, cols(c)]))
        h = rs_done() + (x0(me, mine) if l == 0 else xs[...])
        hs[l] = h
        ag_send(norm(h, g_of(l, 1), b_of(l, 1)).astype(BF16).astype(F32))

        def up_block(b, r, l=l):
            mlp_up(l, r, ag[r].astype(BF16))
        ag_take(up_block)
        if l == 0:
            rs_send(lambda r, c: nn(act[0, r], wdown_ref[0, :, cols(c)]))
            x1 = rs_done() + hs[0]
            xs[...] = x1
            ag_send(norm(x1, g_of(1, 0), b_of(1, 0)).astype(BF16).astype(F32))

    carry[...] = cot_ref[mine].astype(F32)
    for l in (1, 0):
        gmat = gm1_ref if l == 1 else gm0_ref
        gatt = ga1_ref if l == 1 else ga0_ref
        if l == 1:
            each(lambda b, r: mlp_back(1, r, cot_ref[r]))
            glow = cot_ref
        else:
            def back_block(b, r):
                gl = ag[r].astype(BF16)
                low[r] = gl
                mlp_back(0, r, gl)
            ag_take(back_block)
            glow = low
        rs_send(lambda r, c, l=l: nt(du[r], wup_ref[l, cols(c), :]))
        weight_grad_wide(act.at[l], glow, gmat.at[1])
        weight_grad_wide(n2.at[l], du, gmat.at[0])
        dx, gg, bg = norm_back(rs_done(), hs[l], g_of(l, 1))
        vec_add(l, 1, gg, bg)
        dh = carry[...] + dx
        carry[...] = dh
        ag_send(dh.astype(BF16).astype(F32))

        def attn_back_block(b, r, l=l):
            dl = ag[r].astype(BF16)
            low[r] = dl
            attn_back(l, b, r, nt(dl, wout_ref[l]).astype(BF16))
        ag_take(attn_back_block)
        rs_send(lambda r, c, l=l: nn(dq[r], wqkv_ref[l, 0:192, cols(c)]) + nn(dk[r], wqkv_ref[l, 192:384, cols(c)])
                + nn(dv[r], wqkv_ref[l, 384:576, cols(c)]))
        for i, t in enumerate((dq, dk, dv)):
            weight_grad(t, n1.at[l], gatt.at[0], 192, 192 * i)
        weight_grad(o.at[l], low, gatt.at[0], 192, 576)
        dx, gg, bg = norm_back(rs_done(), xs[...] if l == 1 else x0(me, mine), g_of(l, 0))
        vec_add(l, 0, gg, bg)
        g = carry[...] + dx
        carry[...] = g
        if l == 1:
            ag_send(g.astype(BF16).astype(F32))
    ag_send(carry[...])

    def grad_block(b, r):
        tg_ref[r] = ag[r]
    ag_take(grad_block)

    rs_send(lambda r, c: nn(act[1, r], wdown_ref[1, :, cols(c)]))
    ag_send((rs_done() + hs[1]).astype(BF16).astype(F32))

    def out_block(b, r):
        lo_ref[r] = ag[r].astype(BF16)
    ag_take(out_block)


def on_device(nz, ny, nx, tokens, cotangent, buckets, time_table, w_qkv, w_out, w_up, w_down, norm_gain, norm_bias):
    trow = jnp.take(time_table, buckets, axis=0).astype(F32).reshape(-1, 1, D)
    wqkv = w_qkv.transpose(0, 2, 3, 1).reshape(2, -1, D)
    vm = pl.BlockSpec(memory_space=pltpu.VMEM)
    sd = jax.ShapeDtypeStruct
    sem = pltpu.SemaphoreType.DMA
    out = pl.pallas_call(
        functools.partial(body, nz, ny, nx),
        out_shape=(sd((ROWS, D), BF16), sd((ROWS, D), F32), sd((2, D, D), F32), sd((1, D, D), F32),
                   sd((2, D, D), F32), sd((1, D, D), F32), sd((8, D), F32)),
        in_specs=[vm] * 9,
        out_specs=(vm,) * 7,
        scratch_shapes=[
            pltpu.VMEM((ROWS, D), F32),
            pltpu.VMEM((4, BLK, D), F32),
            pltpu.VMEM((2, HALF, D), F32),
            pltpu.VMEM((2, BLK, D), F32),
            pltpu.VMEM((2, ROWS, D), BF16),
            pltpu.VMEM((2, ROWS, D), BF16),
            pltpu.VMEM((2, ROWS, D), BF16),
            pltpu.VMEM((2, ROWS, 192), BF16),
            pltpu.VMEM((2, ROWS, 192), BF16),
            pltpu.VMEM((2, ROWS, 192), BF16),
            pltpu.VMEM((2, ROWS, 192), BF16),
            pltpu.VMEM((2, ROWS, D), F32),
            pltpu.VMEM((2, 12, BLK, BLK), F32),
            pltpu.VMEM((2, BLK, D), F32),
            pltpu.VMEM((BLK, D), F32),
            pltpu.VMEM((BLK, D), F32),
            pltpu.VMEM((ROWS, D), BF16),
            pltpu.VMEM((ROWS, D), BF16),
            pltpu.VMEM((ROWS, 192), BF16),
            pltpu.VMEM((ROWS, 192), BF16),
            pltpu.VMEM((ROWS, 192), BF16),
            sem((6,)), sem((6,)), sem((6,)), sem((6,)),
        ],
        compiler_params=pltpu.CompilerParams(collective_id=0, has_side_effects=True, vmem_limit_bytes=60 * 2 ** 20),
        name="layers",
    )(tokens, trow, cotangent, wqkv, w_out, w_up, w_down, norm_gain.reshape(4, D), norm_bias.reshape(4, D))
    lo, tg, gm1, ga1, gm0, ga0, vec = out
    mats = jnp.concatenate([ga0, gm0, ga1, gm1])
    mats = lax.psum(mats, "dp")
    vec = lax.psum(vec, ("dp", "tensor"))
    col = lax.axis_index("tensor") * 192
    sums = jnp.sum(tg.reshape(-1, SEQ_LEN, D), axis=1)
    sums = lax.dynamic_slice_in_dim(sums, col, 192, 1)
    sums = lax.all_gather(sums, "dp", axis=0, tiled=True)
    ids = lax.all_gather(buckets, "dp", axis=0, tiled=True)
    onehot = (ids[:, None] == jnp.arange(time_table.shape[0], dtype=jnp.int32)[None, :]).astype(F32)
    table = jnp.einsum("sb,sd->bd", onehot, sums, precision=lax.Precision.HIGHEST)
    att = jnp.stack([mats[0], mats[3]])
    up = jnp.stack([mats[1], mats[4]])
    down = jnp.stack([mats[2], mats[5]])
    qkv = att[:, 0:576].reshape(2, 3, 192, D).transpose(0, 3, 1, 2)
    return (lo, tg, table, qkv, att[:, 576:768], up, down, vec[0:4].reshape(2, 2, D), vec[4:8].reshape(2, 2, D))


def solution(mesh):
    placed = (
        P("dp", None), P("dp", None), P("dp"), P(), P(None, None, None, "tensor"), P(None, "tensor", None),
        P(None, None, "tensor"), P(None, "tensor", None), P(), P(),
    )
    return jax.shard_map(
        functools.partial(on_device, 4, 4, 4),
        mesh=mesh,
        in_specs=placed,
        out_specs=(
            P("dp", None), P("dp", None), P(None, "tensor"), P(None, None, None, "tensor"), P(None, "tensor", None),
            P(None, None, "tensor"), P(None, "tensor", None), P(), P(),
        ),
        check_vma=False,
    )
```

```python
import functools

import jax
import jax.numpy as jnp
from jax import lax
from jax.experimental import pallas as pl
from jax.experimental.pallas import tpu as pltpu
from jax.sharding import PartitionSpec as P

MESH = pl.DeviceIdType.MESH
F32 = jnp.float32
BF16 = jnp.bfloat16
HEAD_DIM = 64
SEQ_LEN = 64
D = 768
ROWS = 512
BLK = 128
HALF = 64
COLS = 256
EPS = 1e-05
GELU_A = 0.7978845608028654
GELU_B = 0.044715


def nn(a, b):
    return lax.dot_general(a, b, (((1,), (0,)), ((), ())), preferred_element_type=F32)


def nt(a, b):
    return lax.dot_general(a, b, (((1,), (1,)), ((), ())), preferred_element_type=F32)


def tn(a, b):
    return lax.dot_general(a, b, (((0,), (0,)), ((), ())), preferred_element_type=F32)


def norm_parts(x):
    c = x - jnp.mean(x, axis=-1, keepdims=True)
    r = lax.rsqrt(jnp.mean(c * c, axis=-1, keepdims=True) + EPS)
    return c * r, r


def norm(x, g, b):
    return norm_parts(x)[0] * g + b


def norm_back(dn, x, g):
    xh, r = norm_parts(x)
    dx = dn * g
    dx = r * (dx - jnp.mean(dx, axis=-1, keepdims=True) - xh * jnp.mean(dx * xh, axis=-1, keepdims=True))
    return dx, jnp.sum(dn * xh, axis=0, keepdims=True), jnp.sum(dn, axis=0, keepdims=True)


def gelu_cdf(u):
    t = jnp.tanh(GELU_A * (u + GELU_B * (u * u * u)))
    return t, 0.5 + 0.5 * t


def gelu(u):
    return u * gelu_cdf(u)[1]


def gelu_slope(u):
    t, cdf = gelu_cdf(u)
    return cdf + u * (0.5 * (1.0 - t * t)) * (GELU_A * (1.0 + 3.0 * GELU_B * (u * u)))


def body(nz, ny, nx,
         tok_ref, trow_ref, cot_ref, ids_ref, wqkv_ref, wout_ref, wup_ref, wdown_ref, gain_ref, bias_ref,
         lo_ref, tg_ref, table_ref, gain_out, bias_out, att_out, mlp_out,
         gm1_ref, ga1_ref, gm0_ref, ga0_ref, vec_ref, ag, sbuf, rh, rf, n1, n2, act, q, k, v, o, u, prob, hs, xs, carry, low, du, dq, dk, dv,
         core_m, half_m, full_m, sub_m, core_a, half_a, full_a, sub_a, vecs, ids_all, sums_all,
         rs_s, rs_r, ag_s, ag_r, sm_s, sm_r, sa_s, sa_r, sv_s, sv_r, si_s, si_r, st_s, st_r, km_s, ka_s):
    dp = lax.axis_index("dp")
    me = lax.axis_index("tensor")
    core = lax.rem(dp, 2)
    y = lax.rem(dp // 2, ny)
    z = dp // (2 * ny)
    right = (dp, lax.rem(me + 1, nx))
    left = (dp, lax.rem(me + nx - 1, nx))

    def at(zz, yy, cc):
        return ((lax.rem(zz, nz) * ny + lax.rem(yy, ny)) * 2 + lax.rem(cc, 2), me)

    def along(axis, o):
        return at(z, y + o, core) if axis == 0 else at(z + o, y, core)

    twin = at(z, y, core + 1)

    bar = pltpu.get_barrier_semaphore()
    peers = [(dp, lax.rem(me + i, nx)) for i in (1, 2, 3)] + [along(a, i) for a in (0, 1) for i in (1, 2, 3)] + [twin]
    for peer in peers:
        pl.semaphore_signal(bar, inc=1, device_id=peer, device_id_type=MESH)
    pl.semaphore_wait(bar, len(peers))

    def rows(b):
        return pl.ds(pl.multiple_of(b * BLK, BLK), BLK)

    def half(b, i):
        return pl.ds(pl.multiple_of(b * BLK + i * HALF, HALF), HALF)

    def turn(rel):
        return lax.rem(me + rel, nx)

    mine = rows(me)

    def rs_copy(i):
        src, dst, to = [
            (sbuf.at[0, 0:HALF], rh.at[0], right),
            (sbuf.at[0, HALF:BLK], rh.at[1], left),
            (sbuf.at[1, HALF:BLK], rf.at[0, HALF:BLK], right),
            (sbuf.at[2, 0:HALF], rf.at[1, 0:HALF], left),
            (sbuf.at[1, 0:HALF], rf.at[0, 0:HALF], right),
            (sbuf.at[2, HALF:BLK], rf.at[1, HALF:BLK], left),
        ][i]
        return pltpu.make_async_remote_copy(
            src_ref=src, dst_ref=dst, send_sem=rs_s.at[i], recv_sem=rs_r.at[i], device_id=to, device_id_type=MESH)

    def rs_send(part):
        def step(j, _):
            blk = turn(jnp.where(j == 0, 2, jnp.where(j == 1, 1, jnp.where(j == 2, 3, 0))))
            for c in range(D // COLS):
                sbuf[j, :, c * COLS:(c + 1) * COLS] = part(rows(blk), c)

            @pl.when(j == 0)
            def _():
                rs_copy(0).start()
                rs_copy(1).start()

            @pl.when(j == 1)
            def _():
                rs_copy(2).start()

            @pl.when(j == 2)
            def _():
                rs_copy(3).start()
                rs_copy(0).wait_recv()
                sbuf[1, 0:HALF] += rh[0]
                rs_copy(4).start()
                rs_copy(1).wait_recv()
                sbuf[2, HALF:BLK] += rh[1]
                rs_copy(5).start()
            return 0
        lax.fori_loop(0, nx, step, 0)

    def rs_done():
        for i in range(2, 6):
            rs_copy(i).wait_recv()
        total = sbuf[3] + rf[0] + rf[1]
        for i in range(6):
            rs_copy(i).wait_send()
        return total

    def ag_copy(i, arriving=False):
        if arriving:
            b, h = [(3, 0), (1, 1), (3, 1), (1, 0), (2, 0), (2, 1)][i]
        else:
            b, h = [(0, 0), (0, 1), (0, 1), (0, 0), (3, 0), (1, 1)][i]
        at = half(turn(b), h)
        return pltpu.make_async_remote_copy(
            src_ref=ag.at[at], dst_ref=ag.at[at], send_sem=ag_s.at[i], recv_sem=ag_r.at[i],
            device_id=[right, left][i % 2], device_id_type=MESH)

    def ag_send(val):
        ag[mine] = val
        for i in range(4):
            ag_copy(i).start()

    def ag_take(fn):
        def step(j, _):
            blk = turn(jnp.where(j == 0, 0, jnp.where(j == 1, 3, jnp.where(j == 2, 1, 2))))

            @pl.when(j == 1)
            def _():
                ag_copy(0, True).wait_recv()
                ag_copy(4).start()
                ag_copy(1, True).wait_recv()
                ag_copy(5).start()
                ag_copy(2, True).wait_recv()

            @pl.when(j == 2)
            def _():
                ag_copy(3, True).wait_recv()

            @pl.when(j == 3)
            def _():
                ag_copy(4, True).wait_recv()
                ag_copy(5, True).wait_recv()
            fn(blk, rows(blk))
            return 0
        lax.fori_loop(0, nx, step, 0)
        for i in range(6):
            ag_copy(i).wait_send()

    def each(fn):
        def step(j, _):
            fn(j, rows(j))
            return 0
        lax.fori_loop(0, nx, step, 0)

    def g_of(l, i):
        return gain_ref[l, i:i + 1, :]

    def b_of(l, i):
        return bias_ref[l, i:i + 1, :]

    def x0(b, r):
        x = tok_ref[r].astype(F32)
        s = lax.broadcasted_iota(jnp.int32, (BLK, 1), 0) < SEQ_LEN
        return x + jnp.where(s, trow_ref[2 * b], trow_ref[2 * b + 1])

    iq = lax.broadcasted_iota(jnp.int32, (BLK, BLK), 0) // SEQ_LEN
    ik = lax.broadcasted_iota(jnp.int32, (BLK, BLK), 1) // SEQ_LEN
    same = iq == ik
    lane = lax.broadcasted_iota(jnp.int32, (1, BLK), 1) // HEAD_DIM
    heads = [(slice(0, 128), (lane == 0).astype(F32).astype(BF16)), (slice(0, 128), (lane == 1).astype(F32).astype(BF16)),
             (slice(128, 192), None)]

    def only(x, m):
        return x if m is None else x * m

    def attn_out(l, b, r):
        outs = []
        for i, (c, m) in enumerate(heads):
            s = nt(only(q[l, r, c], m), k[l, r, c]) * HEAD_DIM ** -0.5
            s = jnp.where(same, s, -1e30)
            e = jnp.exp(s - jnp.max(s, axis=-1, keepdims=True))
            p = e / jnp.sum(e, axis=-1, keepdims=True)
            prob[l, 3 * b + i] = p
            outs.append(nn(p.astype(BF16), only(v[l, r, c], m)))
        o[l, r, 0:128] = (outs[0] + outs[1]).astype(BF16)
        o[l, r, 128:192] = outs[2].astype(BF16)

    def qkv_attn(l, b, r, n):
        n1[l, r] = n
        for i, t in enumerate((q, k, v)):
            t[l, r, :] = nt(n, wqkv_ref[l, 192 * i:192 * (i + 1), :]).astype(BF16)
        attn_out(l, b, r)

    def attn_back(l, b, r, do):
        got = []
        for i, (c, m) in enumerate(heads):
            p = prob[l, 3 * b + i]
            pb = p.astype(BF16)
            d = only(do[:, c], m)
            dp_ = nt(d, v[l, r, c])
            ds = (p * (dp_ - jnp.sum(p * dp_, axis=-1, keepdims=True))).astype(BF16)
            got.append((nn(ds, only(k[l, r, c], m)), tn(ds, only(q[l, r, c], m)), tn(pb, d)))
        for t, j, s in ((dq, 0, HEAD_DIM ** -0.5), (dk, 1, HEAD_DIM ** -0.5), (dv, 2, 1.0)):
            t[r, 0:128] = ((got[0][j] + got[1][j]) * s).astype(BF16)
            t[r, 128:192] = (got[2][j] * s).astype(BF16)

    def mlp_up(l, r, n):
        n2[l, r] = n
        for c in range(D // COLS):
            cs = slice(c * COLS, (c + 1) * COLS)
            up = nn(n, wup_ref[l, :, cs])
            u[l, r, cs] = up
            act[l, r, cs] = gelu(up).astype(BF16)

    def mlp_back(l, r, gl):
        for c in range(D // COLS):
            cs = slice(c * COLS, (c + 1) * COLS)
            da = nt(gl, wdown_ref[l, cs, :])
            du[r, cs] = (da * gelu_slope(u[l, r, cs])).astype(BF16)

    def weight_grad(a, b, out, wide, at=0):
        for m in range(0, wide, 192):
            for c in range(D // COLS):
                cs = slice(c * COLS, (c + 1) * COLS)
                out[at + m:at + m + 192, cs] = tn(a[:, m:m + 192], b[:, cs])

    def weight_grad_wide(a, b, out):
        def step(i, _):
            at = pl.ds(pl.multiple_of(i * COLS, COLS), COLS)
            for c in range(D // COLS):
                cs = slice(c * COLS, (c + 1) * COLS)
                out[at, cs] = tn(a[:, at], b[:, cs])
            return 0
        lax.fori_loop(0, D // COLS, step, 0)

    def cols(c):
        return slice(c * COLS, (c + 1) * COLS)

    def vec_add(l, i, gg, bg):
        vec_ref[2 * l + i:2 * l + i + 1, :] = gg
        vec_ref[4 + 2 * l + i:5 + 2 * l + i, :] = bg

    def remote(src, dst, sems, i, to):
        return pltpu.make_async_remote_copy(
            src_ref=src, dst_ref=dst, send_sem=sems[0].at[i], recv_sem=sems[1].at[i], device_id=to, device_id_type=MESH)

    def add_into(mat, n, row, count, cs, srcs, unit=48):
        unit = min(unit, count)

        def step(i, _):
            for kk in range(n):
                to = pl.ds(pl.multiple_of(row + i * unit, 8), unit)
                fr = pl.ds(pl.multiple_of(i * unit, 8), unit)
                acc = mat[kk, to, cs]
                for src in srcs:
                    acc = acc + src[kk, fr, :]
                mat[kk, to, cs] = acc
            return 0
        if count == unit:
            step(0, 0)
        else:
            lax.fori_loop(0, count // unit, step, 0)

    def all_sum(mat, res, n, core_b, half_b, full_b, sub_b, sems):
        mine_at = core * 384
        first = (y, z)
        second = (z, y)
        cs = (slice(0, 384), slice(384, 768))

        def blk(p, o, h=0):
            return mine_at + lax.rem(first[p] + o, 4) * 96 + h * 48

        def sub(p, o):
            return blk(p, 0) + lax.rem(second[p] + o, 4) * 24

        def part(p, row, count, of=mat):
            return of.at[:, pl.ds(pl.multiple_of(row, 8), count), cs[p]]

        def copy(p, i):
            s_ = 2 + 18 * p + i
            r_, l_ = along(p, 1), along(p, 3)
            if i < 6:
                src, dst, to = [
                    (part(p, blk(p, 2, 0), 48), half_b.at[p, 0], r_),
                    (part(p, blk(p, 2, 1), 48), half_b.at[p, 1], l_),
                    (part(p, blk(p, 1, 1), 48), full_b.at[p, 0, :, 48:96], r_),
                    (part(p, blk(p, 3, 0), 48), full_b.at[p, 1, :, 0:48], l_),
                    (part(p, blk(p, 1, 0), 48), full_b.at[p, 0, :, 0:48], r_),
                    (part(p, blk(p, 3, 1), 48), full_b.at[p, 1, :, 48:96], l_),
                ][i]
            elif i < 9:
                o_ = i - 5
                src, dst, to = part(p, sub(p, o_), 24), sub_b.at[p, o_ - 1], along(1 - p, o_)
            elif i < 12:
                src, dst = part(p, sub(p, 0), 24), part(p, sub(p, 0), 24, res)
                to = along(1 - p, i - 8)
            else:
                b, h, to = [(0, 0, r_), (0, 1, l_), (0, 1, r_), (0, 0, l_), (3, 0, r_), (1, 1, l_)][i - 12]
                src = dst = part(p, blk(p, b, h), 48, res)
            return remote(src, dst, sems, s_, to)

        def landing(p, i):
            if i < 9:
                return copy(p, i)
            if i < 12:
                ref = part(p, sub(p, 12 - i), 24, res)
            else:
                b, h = [(3, 0), (1, 1), (3, 1), (1, 0), (2, 0), (2, 1)][i - 12]
                ref = part(p, blk(p, b, h), 48, res)
            return remote(ref, ref, sems, 2 + 18 * p + i, along(p, 1))

        def own(o, of=mat):
            return of.at[:, pl.ds(pl.multiple_of(lax.rem(core + o, 2) * 384, 8), 384), :]

        def keep(p):
            return pltpu.make_async_copy(part(p, sub(p, 0), 24), part(p, sub(p, 0), 24, res), sems[2].at[p])

        c0 = remote(own(1), core_b, sems, 0, twin)
        c0.start()
        yield
        c0.wait_recv()
        add_into(mat, n, mine_at, 384, slice(0, 768), [core_b])
        for i in range(4):
            for p in (0, 1):
                copy(p, i).start()
        yield
        for p in (0, 1):
            landing(p, 0).wait_recv()
            add_into(mat, n, blk(p, 1, 0), 48, cs[p], [half_b.at[p, 0]])
            copy(p, 4).start()
            landing(p, 1).wait_recv()
            add_into(mat, n, blk(p, 3, 1), 48, cs[p], [half_b.at[p, 1]])
            copy(p, 5).start()
        yield
        for p in (0, 1):
            for i in (2, 3, 4, 5):
                landing(p, i).wait_recv()
            add_into(mat, n, blk(p, 0), 96, cs[p], [full_b.at[p, 0], full_b.at[p, 1]])
            for i in (6, 7, 8):
                copy(p, i).start()
        c0.wait_send()
        yield
        for p in (0, 1):
            for i in (6, 7, 8):
                landing(p, i).wait_recv()
            add_into(mat, n, sub(p, 0), 24, cs[p], [sub_b.at[p, 0], sub_b.at[p, 1], sub_b.at[p, 2]])
            for i in (9, 10, 11):
                copy(p, i).start()
            keep(p).start()
            for i in range(9):
                copy(p, i).wait_send()
        yield
        for p in (0, 1):
            keep(p).wait()
            for i in (9, 10, 11):
                landing(p, i).wait_recv()
            for i in (12, 13, 14, 15):
                copy(p, i).start()
        yield
        for p in (0, 1):
            landing(p, 12).wait_recv()
            copy(p, 16).start()
            landing(p, 13).wait_recv()
            copy(p, 17).start()
        yield
        for p in (0, 1):
            for i in (14, 15, 16, 17):
                landing(p, i).wait_recv()
        c1 = remote(own(0, res), own(0, res), sems, 1, twin)
        c1.start()
        for p in (0, 1):
            for i in range(9, 18):
                copy(p, i).wait_send()
        yield
        remote(own(1, res), own(1, res), sems, 1, twin).wait_recv()
        c1.wait_send()

    running = []

    def tick():
        for t in list(running):
            if next(t, True):
                running.remove(t)

    def finish(t):
        while t in running:
            if next(t, True):
                running.remove(t)

    def spread(buf, sems):
        def group(i):
            if i < 3:
                return buf.at[z, y, core], along(1, i + 1), lambda: buf.at[lax.rem(z + 3 - i, 4), y, core]
            if i < 6:
                return buf.at[:, y, core], along(0, i - 2), lambda: buf.at[:, lax.rem(y + 6 - i, 4), core]
            return buf.at[:, :, core], twin, lambda: buf.at[:, :, lax.rem(core + 1, 2)]

        for some in ((0, 1, 2), (3, 4, 5), (6,)):
            for i in some:
                src, to, _ = group(i)
                remote(src, src, sems, i, to).start()
            yield
            for i in some:
                src, to, where = group(i)
                remote(where(), where(), sems, i, to).wait_recv()
            for i in some:
                src, to, _ = group(i)
                remote(src, src, sems, i, to).wait_send()

    def sum_vecs():
        val = vec_ref[...]
        i = 0
        for stage, (pos, peers_) in enumerate((
                (me, [(dp, lax.rem(me + i_, nx)) for i_ in (1, 2, 3)]),
                (z, [along(1, i_) for i_ in (1, 2, 3)]),
                (y, [along(0, i_) for i_ in (1, 2, 3)]),
                (core, [twin]))):
            count = len(peers_) + 1
            buf = vecs.at[stage]
            buf[pos] = val
            sent = []
            for j, to in enumerate(peers_):
                cp = remote(buf.at[pos], buf.at[pos], (sv_s, sv_r), i + j, to)
                cp.start()
                sent.append(cp)
            yield
            for j in range(len(peers_)):
                ref = buf.at[lax.rem(pos + count - 1 - j, count)]
                remote(ref, ref, (sv_s, sv_r), i + j, twin).wait_recv()
            for cp in sent:
                cp.wait_send()
            i += len(peers_)
            val = buf[0]
            for j in range(1, count):
                val = val + buf[j]
        for l in range(2):
            for w in range(2):
                gain_out[l, w:w + 1, :] = val[2 * l + w:2 * l + w + 1, :]
                bias_out[l, w:w + 1, :] = val[4 + 2 * l + w:5 + 2 * l + w, :]

    def table_sums():
        bound = table_ref.shape[1]
        ids = ids_all[...].reshape(256, BLK)[:, 0:1]
        rest = jnp.zeros((256, 192), F32)
        flat = sums_all[...].reshape(256, D)
        for t in range(4):
            rest = jnp.where(me == t, flat[:, 192 * t:192 * (t + 1)], rest)
        parts = []
        for _ in range(3):
            top = rest.astype(BF16)
            parts.append(top)
            rest = rest - top.astype(F32)
        for c in range(0, bound, 512):
            w = min(512, bound - c)
            hot = lax.broadcasted_iota(jnp.int32, (256, w), 1).astype(F32) + float(c) == ids
            hot = hot.astype(F32).astype(BF16)
            table_ref[:, c:c + w] = tn(parts[0], hot) + (tn(parts[1], hot) + tn(parts[2], hot))

    ids_all[z, y, core] = ids_ref[...].astype(F32)
    running.append(spread(ids_all, (si_s, si_r)))
    tick()
    def first(b, r):
        qkv_attn(0, b, r, norm(x0(b, r), g_of(0, 0), b_of(0, 0)).astype(BF16))
    each(first)
    x_own = x0(me, mine)
    for l in range(2):
        if l == 1:
            def attn_block(b, r):
                qkv_attn(1, b, r, ag[r].astype(BF16))
            ag_take(attn_block)
        rs_send(lambda r, c, l=l: nn(o[l, r], wout_ref[l, :, cols(c)]))
        h = rs_done() + (x0(me, mine) if l == 0 else xs[...])
        hs[l] = h
        ag_send(norm(h, g_of(l, 1), b_of(l, 1)).astype(BF16).astype(F32))

        def up_block(b, r, l=l):
            mlp_up(l, r, ag[r].astype(BF16))
        ag_take(up_block)
        if l == 0:
            rs_send(lambda r, c: nn(act[0, r], wdown_ref[0, :, cols(c)]))
            x1 = rs_done() + hs[0]
            xs[...] = x1
            ag_send(norm(x1, g_of(1, 0), b_of(1, 0)).astype(BF16).astype(F32))

    carry[...] = cot_ref[mine].astype(F32)
    mlp_sum = att_sum = None
    for l in (1, 0):
        gmat = gm1_ref if l == 1 else gm0_ref
        gatt = ga1_ref if l == 1 else ga0_ref
        if l == 1:
            each(lambda b, r: mlp_back(1, r, cot_ref[r]))
            glow = cot_ref
        else:
            def back_block(b, r):
                gl = ag[r].astype(BF16)
                low[r] = gl
                mlp_back(0, r, gl)
            ag_take(back_block)
            glow = low
        tick()
        rs_send(lambda r, c, l=l: nt(du[r], wup_ref[l, cols(c), :]))
        tick()
        weight_grad_wide(act.at[l], glow, gmat.at[1])
        weight_grad_wide(n2.at[l], du, gmat.at[0])
        finish(mlp_sum)
        mlp_sum = all_sum(gmat, mlp_out.at[l], 2, core_m, half_m, full_m, sub_m, (sm_s, sm_r, km_s))
        running.append(mlp_sum)
        tick()
        dx, gg, bg = norm_back(rs_done(), hs[l], g_of(l, 1))
        vec_add(l, 1, gg, bg)
        dh = carry[...] + dx
        carry[...] = dh
        ag_send(dh.astype(BF16).astype(F32))
        tick()

        def attn_back_block(b, r, l=l):
            dl = ag[r].astype(BF16)
            low[r] = dl
            attn_back(l, b, r, nt(dl, wout_ref[l]).astype(BF16))
        ag_take(attn_back_block)
        tick()
        rs_send(lambda r, c, l=l: nn(dq[r], wqkv_ref[l, 0:192, cols(c)]) + nn(dk[r], wqkv_ref[l, 192:384, cols(c)])
                + nn(dv[r], wqkv_ref[l, 384:576, cols(c)]))
        tick()
        for i, t in enumerate((dq, dk, dv)):
            weight_grad(t, n1.at[l], gatt.at[0], 192, 192 * i)
        weight_grad(o.at[l], low, gatt.at[0], 192, 576)
        finish(att_sum)
        att_sum = all_sum(gatt, att_out.at[l], 1, core_a, half_a, full_a, sub_a, (sa_s, sa_r, ka_s))
        running.append(att_sum)
        tick()
        dx, gg, bg = norm_back(rs_done(), xs[...] if l == 1 else x0(me, mine), g_of(l, 0))
        vec_add(l, 0, gg, bg)
        g = carry[...] + dx
        carry[...] = g
        if l == 1:
            ag_send(g.astype(BF16).astype(F32))
            tick()
    ag_send(carry[...])
    running.append(sum_vecs())
    tick()

    def grad_block(b, r):
        g = ag[r]
        tg_ref[r] = g
        for i in range(2):
            sums_all[z, y, core, pl.ds(2 * b + i, 1), :] = jnp.sum(g[SEQ_LEN * i:SEQ_LEN * (i + 1)], axis=0, keepdims=True)
    ag_take(grad_block)
    running.append(spread(sums_all, (st_s, st_r)))
    tick()
    rs_send(lambda r, c: nn(act[1, r], wdown_ref[1, :, cols(c)]))
    tick()
    ag_send((rs_done() + hs[1]).astype(BF16).astype(F32))
    tick()

    def out_block(b, r):
        lo_ref[r] = ag[r].astype(BF16)
    ag_take(out_block)
    tick()
    tick()
    table_sums()
    while running:
        tick()


def on_device(nz, ny, nx, tokens, cotangent, buckets, time_table, w_qkv, w_out, w_up, w_down, norm_gain, norm_bias):
    trow = jnp.take(time_table, buckets, axis=0).astype(F32).reshape(-1, 1, D)
    ids = jnp.broadcast_to(buckets[:, None], (buckets.shape[0], BLK))
    wqkv = w_qkv.transpose(0, 2, 3, 1).reshape(2, -1, D)
    vm = pl.BlockSpec(memory_space=pltpu.VMEM)
    hbm = pl.BlockSpec(memory_space=pl.ANY)
    sd = jax.ShapeDtypeStruct
    sem = pltpu.SemaphoreType.DMA

    def sum_bufs(n):
        return [
            pltpu.VMEM((n, 384, D), F32),
            pltpu.VMEM((2, 2, n, 48, 384), F32),
            pltpu.VMEM((2, 2, n, 96, 384), F32),
            pltpu.VMEM((2, 3, n, 24, 384), F32),
        ]

    lo, tg, table, gain, bias, att, mlp = pl.pallas_call(
        functools.partial(body, nz, ny, nx),
        out_shape=(sd((ROWS, D), BF16), sd((ROWS, D), F32), sd((192, time_table.shape[0]), F32),
                   sd((2, 2, D), F32), sd((2, 2, D), F32),
                   sd((2, 1, D, D), F32), sd((2, 2, D, D), F32)),
        in_specs=[vm] * 10,
        out_specs=(vm,) * 5 + (hbm,) * 2,
        scratch_shapes=[
            pltpu.VMEM((2, D, D), F32),
            pltpu.VMEM((1, D, D), F32),
            pltpu.VMEM((2, D, D), F32),
            pltpu.VMEM((1, D, D), F32),
            pltpu.VMEM((8, D), F32),
            pltpu.VMEM((ROWS, D), F32),
            pltpu.VMEM((4, BLK, D), F32),
            pltpu.VMEM((2, HALF, D), F32),
            pltpu.VMEM((2, BLK, D), F32),
            pltpu.VMEM((2, ROWS, D), BF16),
            pltpu.VMEM((2, ROWS, D), BF16),
            pltpu.VMEM((2, ROWS, D), BF16),
            pltpu.VMEM((2, ROWS, 192), BF16),
            pltpu.VMEM((2, ROWS, 192), BF16),
            pltpu.VMEM((2, ROWS, 192), BF16),
            pltpu.VMEM((2, ROWS, 192), BF16),
            pltpu.VMEM((2, ROWS, D), F32),
            pltpu.VMEM((2, 12, BLK, BLK), F32),
            pltpu.VMEM((2, BLK, D), F32),
            pltpu.VMEM((BLK, D), F32),
            pltpu.VMEM((BLK, D), F32),
            pltpu.VMEM((ROWS, D), BF16),
            pltpu.VMEM((ROWS, D), BF16),
            pltpu.VMEM((ROWS, 192), BF16),
            pltpu.VMEM((ROWS, 192), BF16),
            pltpu.VMEM((ROWS, 192), BF16),
        ] + sum_bufs(2) + sum_bufs(1) + [
            pltpu.VMEM((4, 4, 8, D), F32),
            pltpu.VMEM((4, 4, 2, 8, BLK), F32),
            pltpu.VMEM((4, 4, 2, 8, D), F32),
            sem((6,)), sem((6,)), sem((6,)), sem((6,)), sem((38,)), sem((38,)), sem((38,)), sem((38,)),
            sem((10,)), sem((10,)), sem((7,)), sem((7,)), sem((7,)), sem((7,)), sem((2,)), sem((2,)),
        ],
        compiler_params=pltpu.CompilerParams(collective_id=0, has_side_effects=True, vmem_limit_bytes=62 * 2 ** 20),
        name="layers",
    )(tokens, trow, cotangent, ids, wqkv, w_out, w_up, w_down, norm_gain, norm_bias)
    qkv = att[:, 0, 0:576].reshape(2, 3, 192, D).transpose(0, 3, 1, 2)
    return (lo, tg, table.T, qkv, att[:, 0, 576:768], mlp[:, 0], mlp[:, 1], gain, bias)


def solution(mesh):
    placed = (
        P("dp", None), P("dp", None), P("dp"), P(), P(None, None, None, "tensor"), P(None, "tensor", None),
        P(None, None, "tensor"), P(None, "tensor", None), P(), P(),
    )
    return jax.shard_map(
        functools.partial(on_device, 4, 4, 4),
        mesh=mesh,
        in_specs=placed,
        out_specs=(
            P("dp", None), P("dp", None), P(None, "tensor"), P(None, None, None, "tensor"), P(None, "tensor", None),
            P(None, None, "tensor"), P(None, "tensor", None), P(), P(),
        ),
        check_vma=False,
    )
```

```python
import functools

import jax
import jax.numpy as jnp
from jax import lax
from jax.experimental import pallas as pl
from jax.experimental.pallas import tpu as pltpu
from jax.sharding import PartitionSpec as P

MESH = pl.DeviceIdType.MESH
F32 = jnp.float32
BF16 = jnp.bfloat16
HEAD_DIM = 64
SEQ_LEN = 64
D = 768
ROWS = 512
BLK = 128
HALF = 64
COLS = 256
EPS = 1e-05
GELU_A = 0.7978845608028654
GELU_B = 0.044715


def nn(a, b):
    return lax.dot_general(a, b, (((1,), (0,)), ((), ())), preferred_element_type=F32)


def nt(a, b):
    return lax.dot_general(a, b, (((1,), (1,)), ((), ())), preferred_element_type=F32)


def tn(a, b):
    return lax.dot_general(a, b, (((0,), (0,)), ((), ())), preferred_element_type=F32)


def norm_parts(x):
    c = x - jnp.mean(x, axis=-1, keepdims=True)
    r = lax.rsqrt(jnp.mean(c * c, axis=-1, keepdims=True) + EPS)
    return c * r, r


def norm(x, g, b):
    return norm_parts(x)[0] * g + b


def norm_back(dn, x, g):
    xh, r = norm_parts(x)
    dx = dn * g
    dx = r * (dx - jnp.mean(dx, axis=-1, keepdims=True) - xh * jnp.mean(dx * xh, axis=-1, keepdims=True))
    return dx, jnp.sum(dn * xh, axis=0, keepdims=True), jnp.sum(dn, axis=0, keepdims=True)


def gelu_cdf(u):
    t = jnp.tanh(GELU_A * (u + GELU_B * (u * u * u)))
    return t, 0.5 + 0.5 * t


def gelu(u):
    return u * gelu_cdf(u)[1]


def gelu_slope(u):
    t, cdf = gelu_cdf(u)
    return cdf + u * (0.5 * (1.0 - t * t)) * (GELU_A * (1.0 + 3.0 * GELU_B * (u * u)))


def body(nz, ny, nx,
         tok_ref, trow_ref, cot_ref, ids_ref, wqkv_ref, wout_ref, wup_ref, wdown_ref, gain_ref, bias_ref,
         lo_out, tg_out, table_out, gain_out, bias_out, att_out, mlp_out, land, core_m, core_a, n1_all, n2_all, da_all,
         gmat, gatt, vec_ref, ag, sbuf, rh, rf, n1, n2, act, q, k, v, o, u, prob, hs, xs, carry, gmlow, low, du, dq, dk, dv,
         watt, wst, acc, acc2, src_x, take_x,
         mine_w, far_w, stage, half_m, full_m, sub_m, half_a, full_a, sub_a, vecs, ids_all, sums_all,
         rs_s, rs_r, ag_s, ag_r, gx_s, gx_r, sm_s, sm_r, sa_s, sa_r, sw_s, sw_r, sv_s, sv_r, si_s, si_r, st_s, st_r,
         keep_s, stage_s, wst_s, take_s, out_s):
    dp = lax.axis_index("dp")
    me = lax.axis_index("tensor")
    core = lax.rem(dp, 2)
    y = lax.rem(dp // 2, ny)
    z = dp // (2 * ny)
    right = (dp, lax.rem(me + 1, nx))
    left = (dp, lax.rem(me + nx - 1, nx))

    def at(zz, yy, cc):
        return ((lax.rem(zz, nz) * ny + lax.rem(yy, ny)) * 2 + lax.rem(cc, 2), me)

    def along(axis, o):
        return at(z, y + o, core) if axis == 0 else at(z + o, y, core)

    twin = at(z, y, core + 1)

    bar = pltpu.get_barrier_semaphore()
    peers = [(dp, lax.rem(me + i, nx)) for i in (1, 2, 3)] + [along(a, i) for a in (0, 1) for i in (1, 2, 3)] + [twin]
    for peer in peers:
        pl.semaphore_signal(bar, inc=1, device_id=peer, device_id_type=MESH)
    pl.semaphore_wait(bar, len(peers))

    def rows(b):
        return pl.ds(pl.multiple_of(b * BLK, BLK), BLK)

    def half(b, i):
        return pl.ds(pl.multiple_of(b * BLK + i * HALF, HALF), HALF)

    def turn(rel):
        return lax.rem(me + rel, nx)

    mine = rows(me)

    now = [0.0]
    free = {"core": 0.0, "yz": 0.0, "x": 0.0}
    running = []

    def work(t):
        now[0] += t

    def link(which, t):
        free[which] = max(now[0], free[which]) + t
        return free[which] + 2.0

    def advance(entry):
        now[0] = max(now[0], entry[1])
        got = next(entry[0], None)
        if got is None:
            running.remove(entry)
        else:
            entry[1], entry[2] = got if isinstance(got, tuple) else (got, 0.3)

    def begin(gen):
        entry = [gen, 0.0, 0.0]
        running.append(entry)
        advance(entry)
        return entry

    def idle(until, late=0.5):
        while True:
            fit = [e for e in running if max(now[0], e[1]) + e[2] <= until + late]
            if not fit:
                break
            advance(min(fit, key=lambda e: (max(now[0], e[1]), e[2])))
        now[0] = max(now[0], until)

    def ready():
        idle(now[0])

    def finish(entry):
        while entry in running:
            advance(min(running, key=lambda e: e[1]))

    def after(which):
        while which not in sums or sums[which] in running:
            yield max(now[0], sums[which][1] if which in sums else 0.0) + 0.5, 0.0

    def rs_copy(i):
        src, dst, to = [
            (sbuf.at[0, 0:HALF], rh.at[0], right),
            (sbuf.at[0, HALF:BLK], rh.at[1], left),
            (sbuf.at[1, HALF:BLK], rf.at[0, HALF:BLK], right),
            (sbuf.at[2, 0:HALF], rf.at[1, 0:HALF], left),
            (sbuf.at[1, 0:HALF], rf.at[0, 0:HALF], right),
            (sbuf.at[2, HALF:BLK], rf.at[1, HALF:BLK], left),
        ][i]
        return pltpu.make_async_remote_copy(
            src_ref=src, dst_ref=dst, send_sem=rs_s.at[i], recv_sem=rs_r.at[i], device_id=to, device_id_type=MESH)

    rs_end = [0.0]

    def rs_send(part, cost):
        began = 0.0
        for j, rel in enumerate((2, 1, 3, 0)):
            r = rows(turn(rel))
            for c in range(D // COLS):
                sbuf[j, :, c * COLS:(c + 1) * COLS] = part(r, c)
            work(cost)
            if j == 0:
                rs_copy(0).start()
                rs_copy(1).start()
                began = link("x", 12.5) - 14.5
            if j == 1:
                rs_copy(2).start()
            if j == 2:
                rs_copy(3).start()
                idle(began + 6.0)
                rs_copy(0).wait_recv()
                sbuf[1, 0:HALF] += rh[0]
                rs_copy(4).start()
                rs_copy(1).wait_recv()
                sbuf[2, HALF:BLK] += rh[1]
                rs_copy(5).start()
                work(0.2)
        rs_end[0] = began + 14.0
        ready()

    def rs_done():
        idle(rs_end[0])
        for i in range(2, 6):
            rs_copy(i).wait_recv()
        total = sbuf[3] + rf[0] + rf[1]
        for i in range(6):
            rs_copy(i).wait_send()
        work(1.0)
        return total

    def ag_copy(i, arriving=False):
        if arriving:
            b, h = [(3, 0), (1, 1), (3, 1), (1, 0), (2, 0), (2, 1)][i]
        else:
            b, h = [(0, 0), (0, 1), (0, 1), (0, 0), (3, 0), (1, 1)][i]
        at = half(turn(b), h)
        return pltpu.make_async_remote_copy(
            src_ref=ag.at[at], dst_ref=ag.at[at], send_sem=ag_s.at[i], recv_sem=ag_r.at[i],
            device_id=[right, left][i % 2], device_id_type=MESH)

    ag_began = [0.0]

    def ag_send(val):
        ag[mine] = val
        for i in range(4):
            ag_copy(i).start()
        ag_began[0] = link("x", 12.5) - 14.5

    def ag_take(fn, cost):
        for j, rel in enumerate((0, 3, 1, 2)):
            blk = turn(rel)
            if j == 1:
                idle(ag_began[0] + 5.7)
                ag_copy(0, True).wait_recv()
                ag_copy(4).start()
                ag_copy(1, True).wait_recv()
                ag_copy(5).start()
                idle(ag_began[0] + 9.9)
                ag_copy(2, True).wait_recv()
            if j == 2:
                ag_copy(3, True).wait_recv()
            if j == 3:
                idle(ag_began[0] + 14.0)
                ag_copy(4, True).wait_recv()
                ag_copy(5, True).wait_recv()
            fn(blk, rows(blk))
            work(cost)
            ready()
        for i in range(6):
            ag_copy(i).wait_send()

    def each(fn, cost):
        def step(j, _):
            fn(j, rows(j))
            return 0
        lax.fori_loop(0, nx // 2, step, 0)
        work(2 * cost)
        ready()
        lax.fori_loop(nx // 2, nx, step, 0)
        work(2 * cost)
        ready()

    def gather_x(w, dst):
        src = src_x.at[w]

        def copy(i, arriving=False):
            if arriving:
                b, h = [(3, 0), (1, 1), (3, 1), (1, 0), (2, 0), (2, 1)][i]
            else:
                b, h = [(0, 0), (0, 1), (0, 1), (0, 0), (3, 0), (1, 1)][i]
            to = dst.at[half(turn(b), h)]
            fr = to if arriving or i > 3 else src.at[h * HALF:(h + 1) * HALF]
            return pltpu.make_async_remote_copy(
                src_ref=fr, dst_ref=to, send_sem=gx_s.at[w, i], recv_sem=gx_r.at[w, i],
                device_id=[right, left][i % 2], device_id_type=MESH)

        for i in range(4):
            copy(i).start()
        keep = pltpu.make_async_copy(src, dst.at[mine], keep_s.at[5 + w])
        keep.start()
        first = link("x", 4.2)
        link("x", 4.2)
        yield first
        copy(0, True).wait_recv()
        copy(4).start()
        copy(1, True).wait_recv()
        copy(5).start()
        yield link("x", 4.2)
        for i in range(2, 6):
            copy(i, True).wait_recv()
        for i in range(6):
            copy(i).wait_send()
        keep.wait()

    def taken(from_ref, fn, cost):
        def fetch(b):
            return pltpu.make_async_copy(from_ref.at[b * BLK:(b + 1) * BLK], take_x.at[b % 2], take_s.at[b % 2])
        fetch(0).start()
        for b in range(4):
            if b < 3:
                fetch(b + 1).start()
            yield now[0], cost
            fetch(b).wait()
            fn(b, slice(b * BLK, (b + 1) * BLK), take_x[b % 2].astype(BF16))
            work(cost)

    def g_of(l, i):
        return gain_ref[l, i:i + 1, :]

    def b_of(l, i):
        return bias_ref[l, i:i + 1, :]

    def x0(b, r):
        x = tok_ref[r].astype(F32)
        s = lax.broadcasted_iota(jnp.int32, (BLK, 1), 0) < SEQ_LEN
        return x + jnp.where(s, trow_ref[2 * b], trow_ref[2 * b + 1])

    iq = lax.broadcasted_iota(jnp.int32, (BLK, BLK), 0) // SEQ_LEN
    ik = lax.broadcasted_iota(jnp.int32, (BLK, BLK), 1) // SEQ_LEN
    same = iq == ik
    lane = lax.broadcasted_iota(jnp.int32, (1, BLK), 1) // HEAD_DIM
    heads = [(slice(0, 128), (lane == 0).astype(F32).astype(BF16)), (slice(0, 128), (lane == 1).astype(F32).astype(BF16)),
             (slice(128, 192), None)]

    def only(x, m):
        return x if m is None else x * m

    def attn_out(qr, kr, vr, o_, pr):
        outs = []
        for i, (c, m) in enumerate(heads):
            s = nt(only(qr[:, c], m), kr[:, c]) * HEAD_DIM ** -0.5
            s = jnp.where(same, s, -1e30)
            e = jnp.exp(s - jnp.max(s, axis=-1, keepdims=True))
            p = e / jnp.sum(e, axis=-1, keepdims=True)
            pr[i] = p
            outs.append(nn(p.astype(BF16), only(vr[:, c], m)))
        o_[:, 0:128] = (outs[0] + outs[1]).astype(BF16)
        o_[:, 128:192] = outs[2].astype(BF16)

    def qkv_attn(l, b, r, n):
        n1[l, r] = n
        for i, t in enumerate((q, k, v)):
            t[l, r, :] = nt(n, wqkv_ref[l, 192 * i:192 * (i + 1), :]).astype(BF16)
        attn_out(q.at[l, r], k.at[l, r], v.at[l, r], o.at[l, r], prob.at[l, pl.ds(3 * b, 3)])

    def qkv_attn_back(l, b, r, dl):
        low[l, r] = dl
        do = nt(dl, wout_ref[l]).astype(BF16)
        attn_back(q.at[l, r], k.at[l, r], v.at[l, r], prob.at[l, pl.ds(3 * b, 3)], do, dq.at[l, r], dk.at[l, r], dv.at[l, r])

    def attn_back(qr, kr, vr, pr, do, dqr, dkr, dvr):
        got = []
        for i, (c, m) in enumerate(heads):
            p = pr[i]
            pb = p.astype(BF16)
            d = only(do[:, c], m)
            dp_ = nt(d, vr[:, c])
            ds = (p * (dp_ - jnp.sum(p * dp_, axis=-1, keepdims=True))).astype(BF16)
            got.append((nn(ds, only(kr[:, c], m)), tn(ds, only(qr[:, c], m)), tn(pb, d)))
        for t, j, s in ((dqr, 0, HEAD_DIM ** -0.5), (dkr, 1, HEAD_DIM ** -0.5), (dvr, 2, 1.0)):
            t[:, 0:128] = ((got[0][j] + got[1][j]) * s).astype(BF16)
            t[:, 128:192] = (got[2][j] * s).astype(BF16)

    def mlp_up(r, n):
        n2[0, r] = n
        for c in range(D // COLS):
            cs = slice(c * COLS, (c + 1) * COLS)
            up = nn(n, wup_ref[0, :, cs])
            u[r, cs] = up
            act[0, r, cs] = gelu(up).astype(BF16)

    def mlp_back(r, gl):
        for c in range(D // COLS):
            cs = slice(c * COLS, (c + 1) * COLS)
            da = nt(gl, wdown_ref[0, cs, :])
            du[0, r, cs] = (da * gelu_slope(u[r, cs])).astype(BF16)

    def mlp_both(n, gl, wu, wd, a_, d_):
        for c in range(D // COLS):
            cs = slice(c * COLS, (c + 1) * COLS)
            up = nn(n, wu[:, cs])
            t, cdf = gelu_cdf(up)
            a_[:, cs] = (up * cdf).astype(BF16)
            slope = cdf + up * (0.5 * (1.0 - t * t)) * (GELU_A * (1.0 + 3.0 * GELU_B * (up * up)))
            d_[:, cs] = (nt(gl, wd[cs, :]) * slope).astype(BF16)

    def weight_grad(a, b, out, at=0):
        for c in range(D // COLS):
            cs = slice(c * COLS, (c + 1) * COLS)
            out[at:at + 192, cs] = tn(a[:, 0:192], b[:, cs])

    def weight_grad_wide(a, b, out):
        def step(i, _):
            at = pl.ds(pl.multiple_of(i * COLS, COLS), COLS)
            for c in range(D // COLS):
                cs = slice(c * COLS, (c + 1) * COLS)
                out[at, cs] = tn(a[:, at], b[:, cs])
            return 0
        lax.fori_loop(0, D // COLS, step, 0)
        work(1.5)

    def cols(c):
        return slice(c * COLS, (c + 1) * COLS)

    def vec_add(l, i, gg, bg):
        vec_ref[2 * l + i:2 * l + i + 1, :] = gg
        vec_ref[4 + 2 * l + i:5 + 2 * l + i, :] = bg

    def remote(src, dst, sems, i, to):
        return pltpu.make_async_remote_copy(
            src_ref=src, dst_ref=dst, send_sem=sems[0].at[i], recv_sem=sems[1].at[i], device_id=to, device_id_type=MESH)

    def shift1(o_):
        return at(z + core * o_, y + (1 - core) * o_, core)

    def shift2(o_):
        return at(z + (1 - core) * o_, y + core * o_, core)

    pos1 = y + core * (z - y)
    pos2 = z + core * (y - z)
    half_cols = pl.ds(pl.multiple_of(core * 384, 128), 384)
    twin_cols = pl.ds(pl.multiple_of((1 - core) * 384, 128), 384)

    def blk(o_, h=0):
        return lax.rem(pos1 + o_, 4) * 192 + h * 96

    def sub(o_):
        return blk(0) + lax.rem(pos2 + o_, 4) * 48

    def part(of, row, count, cs=half_cols):
        return of.at[:, pl.ds(pl.multiple_of(row, 16), count), cs]

    def add_into(mat, n, row, count, srcs, unit=96):
        unit = min(unit, count)

        def step(i, _):
            for kk in range(n):
                to = pl.ds(pl.multiple_of(row + i * unit, 16), unit)
                fr = pl.ds(pl.multiple_of(i * unit, 16), unit)
                val = mat[kk, to, half_cols]
                for src in srcs:
                    val = val + src[kk, fr, :]
                mat[kk, to, half_cols] = val
            return 0
        if count == unit:
            step(0, 0)
        else:
            lax.fori_loop(0, count // unit, step, 0)

    def add_core(mat, n, core_b):
        def fetch(i):
            kk, j = i // 4, i % 4
            return pltpu.make_async_copy(core_b.at[kk, pl.ds(192 * j, 192)], stage.at[i % 2], stage_s.at[i % 2])
        for i in range(2):
            fetch(i).start()
        for i in range(4 * n):
            fetch(i).wait()
            kk, j = i // 4, i % 4
            mat[kk, 192 * j:192 * (j + 1), half_cols] += stage[i % 2]
            if i + 2 < 4 * n:
                fetch(i + 2).start()
        work(0.5 + 0.8 * n)

    def hand_out(src, res, n, sems, keep_s):
        def copy(i):
            if i < 3:
                return remote(src, part(res, sub(0), 48), sems, i, shift2(i + 1))
            b, h, to = [(0, 0, 1), (0, 1, 3), (0, 1, 1), (0, 0, 3), (3, 0, 1), (1, 1, 3)][i - 3]
            ref = part(res, blk(b, h), 96)
            return remote(ref, ref, sems, i, shift1(to))

        def landing(i):
            if i < 3:
                ref = part(res, sub(3 - i), 48)
            else:
                b, h = [(3, 0), (1, 1), (3, 1), (1, 0), (2, 0), (2, 1)][i - 3]
                ref = part(res, blk(b, h), 96)
            return remote(ref, ref, sems, i, twin)

        for i in range(3):
            copy(i).start()
        keep = pltpu.make_async_copy(src, part(res, sub(0), 48), keep_s)
        keep.start()
        yield link("yz", 1.6 * n)
        keep.wait()
        for i in range(3):
            landing(i).wait_recv()
        for i in range(3, 7):
            copy(i).start()
        arrive = link("yz", 1.6 * n)
        link("yz", 1.6 * n)
        yield arrive
        landing(3).wait_recv()
        copy(7).start()
        landing(4).wait_recv()
        copy(8).start()
        yield link("yz", 1.6 * n)
        for i in range(5, 9):
            landing(i).wait_recv()
        last = remote(part(res, 0, D), part(res, 0, D), sems, 9, twin)
        last.start()
        for i in range(9):
            copy(i).wait_send()
        yield link("core", 2.0 * n)
        remote(part(res, 0, D, twin_cols), part(res, 0, D, twin_cols), sems, 9, twin).wait_recv()
        last.wait_send()

    def all_sum(mat, res, n, core_b, half_b, full_b, sub_b, sems, keep_s):
        def copy(i):
            if i < 6:
                src, dst, to = [
                    (part(mat, blk(2, 0), 96), half_b.at[0], 1),
                    (part(mat, blk(2, 1), 96), half_b.at[1], 3),
                    (part(mat, blk(1, 1), 96), full_b.at[0, :, 96:192], 1),
                    (part(mat, blk(3, 0), 96), full_b.at[1, :, 0:96], 3),
                    (part(mat, blk(1, 0), 96), full_b.at[0, :, 0:96], 1),
                    (part(mat, blk(3, 1), 96), full_b.at[1, :, 96:192], 3),
                ][i]
                return remote(src, dst, sems, 10 + i, shift1(to))
            o_ = i - 5
            return remote(part(mat, sub(o_), 48), sub_b.at[o_ - 1], sems, 10 + i, shift2(o_))

        c0 = remote(part(mat, 0, D, twin_cols), core_b, sems, 19, twin)
        c0.start()
        yield link("core", 2.0 * n)
        c0.wait_recv()
        add_core(mat, n, core_b)
        for i in range(4):
            copy(i).start()
        arrive = link("yz", 1.6 * n)
        link("yz", 1.6 * n)
        yield arrive
        copy(0).wait_recv()
        add_into(mat, n, blk(1, 0), 96, [half_b.at[0]])
        copy(4).start()
        copy(1).wait_recv()
        add_into(mat, n, blk(3, 1), 96, [half_b.at[1]])
        copy(5).start()
        work(0.3 * n)
        yield link("yz", 1.6 * n)
        for i in (2, 3, 4, 5):
            copy(i).wait_recv()
        add_into(mat, n, blk(0), 192, [full_b.at[0], full_b.at[1]])
        for i in (6, 7, 8):
            copy(i).start()
        c0.wait_send()
        work(0.5 * n)
        yield link("yz", 1.6 * n)
        for i in (6, 7, 8):
            copy(i).wait_recv()
        add_into(mat, n, sub(0), 48, [sub_b.at[0], sub_b.at[1], sub_b.at[2]])
        for i in range(9):
            copy(i).wait_send()
        work(0.2 * n)
        yield from hand_out(part(mat, sub(0), 48), res, n, sems, keep_s)

    released = [0]

    def fetch_weights(m, fill, use):
        own = mine_w.at[m]
        sems, keep_ = (sw_s.at[m], sw_r.at[m]), keep_s.at[m]
        fill(own)
        sent = [remote(own, far_w.at[m, pl.ds(3 - i, 1)], sems, 9 + i, (dp, lax.rem(me + i, nx))) for i in (1, 2, 3)]
        for cp in sent:
            cp.start()
        yield link("x", 3.2)
        while m > released[0]:
            yield now[0] + 1.0, 0.0
        for cp in sent:
            cp.wait_recv()
        yield from hand_out(far_w.at[m], land.at[m], 3, sems, keep_)
        for cp in sent:
            cp.wait_send()
        use()

    def spread(buf, sems):
        def group(i):
            if i < 3:
                return buf.at[z, y, core], along(1, i + 1), lambda: buf.at[lax.rem(z + 3 - i, 4), y, core]
            if i < 6:
                return buf.at[:, y, core], along(0, i - 2), lambda: buf.at[:, lax.rem(y + 6 - i, 4), core]
            return buf.at[:, :, core], twin, lambda: buf.at[:, :, lax.rem(core + 1, 2)]

        for some in ((0, 1, 2), (3, 4, 5), (6,)):
            for i in some:
                src, to, _ = group(i)
                remote(src, src, sems, i, to).start()
            yield now[0] + 5.0
            for i in some:
                src, to, where = group(i)
                remote(where(), where(), sems, i, to).wait_recv()
            for i in some:
                src, to, _ = group(i)
                remote(src, src, sems, i, to).wait_send()

    def sum_vecs():
        val = vec_ref[...]
        i = 0
        for stage, (pos, peers_) in enumerate((
                (me, [(dp, lax.rem(me + i_, nx)) for i_ in (1, 2, 3)]),
                (z, [along(1, i_) for i_ in (1, 2, 3)]),
                (y, [along(0, i_) for i_ in (1, 2, 3)]),
                (core, [twin]))):
            count = len(peers_) + 1
            buf = vecs.at[stage]
            buf[pos] = val
            sent = []
            for j, to in enumerate(peers_):
                cp = remote(buf.at[pos], buf.at[pos], (sv_s, sv_r), i + j, to)
                cp.start()
                sent.append(cp)
            yield now[0] + 4.0
            for j in range(len(peers_)):
                ref = buf.at[lax.rem(pos + count - 1 - j, count)]
                remote(ref, ref, (sv_s, sv_r), i + j, twin).wait_recv()
            for cp in sent:
                cp.wait_send()
            i += len(peers_)
            val = buf[0]
            for j in range(1, count):
                val = val + buf[j]
        for l in range(2):
            for w in range(2):
                gain_out[l, w:w + 1, :] = val[2 * l + w:2 * l + w + 1, :]
                bias_out[l, w:w + 1, :] = val[4 + 2 * l + w:5 + 2 * l + w, :]

    def table_sums():
        ids = ids_all[...].reshape(256, BLK)[:, 0:1]
        rest = sums_all[...].reshape(256, 256)[:, 0:192]
        parts = []
        for _ in range(3):
            top = rest.astype(BF16)
            parts.append(top)
            rest = rest - top.astype(F32)
        out = []
        for i in range(4):
            hot = lax.broadcasted_iota(jnp.int32, (256, 512), 1).astype(F32) + float(512 * i) == ids
            hot = hot.astype(F32).astype(BF16)
            to = ag.at[0:192, 0:512] if i % 2 == 0 else ag.at[192:384, 0:512]
            if i > 1:
                out[i - 2].wait()
            to[...] = tn(parts[0], hot) + (tn(parts[1], hot) + tn(parts[2], hot))
            cp = pltpu.make_async_copy(to, table_out.at[:, 512 * i:512 * (i + 1)], out_s.at[i])
            cp.start()
            out.append(cp)
        out[2].wait()
        out[3].wait()

    sums = {}

    ids_all[z, y, core] = ids_ref[...].astype(F32)
    begin(spread(ids_all, (si_s, si_r)))
    w_row = pl.multiple_of(sub(0), 16)

    def fill_att(ref):
        @pl.when(w_row < 576)
        def _():
            ref[0] = wqkv_ref[1, pl.ds(w_row, 48), half_cols].astype(F32)

        @pl.when(w_row >= 576)
        def _():
            ref[0] = wout_ref[1, pl.ds(w_row - 576, 48), half_cols].astype(F32)

    def fill_up(ref):
        ref[0] = wup_ref[1, pl.ds(w_row, 48), half_cols].astype(F32)

    def fill_down(ref):
        ref[0] = wdown_ref[1, pl.ds(w_row, 48), half_cols].astype(F32)

    def use_att():
        def fetch(i):
            j, h = i // 2, i % 2
            return pltpu.make_async_copy(land.at[0, j, pl.ds(384 * h, 384)], gmat.at[i % 2, 0:384], wst_s.at[i % 2])
        fetch(0).start()
        for i in range(6):
            if i < 5:
                fetch(i + 1).start()
            fetch(i).wait()
            j, h = i // 2, i % 2
            watt[j, 384 * h:384 * (h + 1)] = gmat[i % 2, 0:384].astype(BF16)
        work(4.0)
    att_weights = begin(fetch_weights(0, fill_att, use_att))
    up_weights = begin(fetch_weights(1, fill_up, lambda: None))
    down_weights = begin(fetch_weights(2, fill_down, lambda: None))

    def first(b, r):
        qkv_attn(0, b, r, norm(x0(b, r), g_of(0, 0), b_of(0, 0)).astype(BF16))
    each(first, 2.2)
    rs_send(lambda r, c: nn(o[0, r], wout_ref[0, :, cols(c)]), 0.4)
    released[0] = 1
    h = rs_done() + x0(me, mine)
    hs[0] = h
    ag_send(norm(h, g_of(0, 1), b_of(0, 1)).astype(BF16).astype(F32))

    def up_block(b, r):
        mlp_up(r, ag[r].astype(BF16))
    ag_take(up_block, 1.0)
    released[0] = 2
    rs_send(lambda r, c: nn(act[0, r], wdown_ref[0, :, cols(c)]), 0.7)
    x1 = rs_done() + hs[0]
    xs[...] = x1

    n1d, lowd, ad, dud = (t.at[1, 0:BLK] for t in (n1, low, act, du))
    dqd, dkd, dvd = (t.at[1, 0:BLK] for t in (dq, dk, dv))

    def shard(t, j):
        return t.at[1, rows(j)]

    def shard_prob(j):
        return prob.at[1, pl.ds(3 * j, 3)]

    n = norm(x1, g_of(1, 0), b_of(1, 0)).astype(BF16)
    n1d[...] = n
    src_x[0] = n.astype(F32)
    sums["n1"] = begin(gather_x(0, n1_all))
    finish(att_weights)

    def local_attn(j, wq, wo):
        for i, t in enumerate((q, k, v)):
            shard(t, j)[...] = nt(n1d[...], wq[192 * i:192 * (i + 1), :]).astype(BF16)
        attn_out(shard(q, j), shard(k, j), shard(v, j), shard(o, j), shard_prob(j))
        for c in range(D // COLS):
            acc[:, cols(c)] += nn(shard(o, j)[...], wo[:, cols(c)])

    def others(fn):
        def step(j, _):
            fn(j + 1, watt.at[j, 0:576], watt.at[j, 576:768])
            return 0
        lax.fori_loop(0, nx - 1, step, 0)

    acc[...] = x1
    local_attn(0, wqkv_ref.at[1], wout_ref.at[1])
    others(local_attn)
    work(7.0)
    ready()
    h = acc[...]
    hs[1] = h
    n = norm(h, g_of(1, 1), b_of(1, 1)).astype(BF16)
    lowd[...] = n
    src_x[1] = n.astype(F32)
    sums["n2"] = begin(gather_x(1, n2_all))
    finish(up_weights)
    finish(down_weights)

    def fetch_mlp(j, w):
        return pltpu.make_async_copy(land.at[1 + w, j], gmat.at[w], wst_s.at[w])

    acc2[...] = jnp.zeros_like(acc2)
    cot_own = cot_ref[mine]
    for w in range(2):
        fetch_mlp(0, w).start()
    for j in range(nx):
        if j == 0:
            wu, wd = wup_ref.at[1], wdown_ref.at[1]
        else:
            wu, wd = wst.at[0], wst.at[1]
            for w in range(2):
                fetch_mlp(j - 1, w).wait()
                wst[w] = gmat[w].astype(BF16)
                if j < nx - 1:
                    fetch_mlp(j, w).start()
        mlp_both(lowd[...], cot_own, wu, wd, ad, dud)
        for c in range(D // COLS):
            acc[:, cols(c)] += nn(ad[...], wd[:, cols(c)])
            acc2[:, cols(c)] += nt(dud[...], wu[cols(c), :])
        work(4.0)
        ready()
    src_x[3] = acc[...].astype(BF16).astype(F32)
    dx, gg, bg = norm_back(acc2[...], hs[1], g_of(1, 1))
    vec_add(1, 1, gg, bg)
    dh = cot_own.astype(F32) + dx
    carry[...] = dh
    lowd[...] = dh.astype(BF16)
    src_x[2] = lowd[...].astype(F32)
    acc[...] = jnp.zeros_like(acc)

    def local_attn_back(j, wq, wo):
        do = nt(lowd[...], wo[...]).astype(BF16)
        attn_back(shard(q, j), shard(k, j), shard(v, j), shard_prob(j), do, dqd, dkd, dvd)
        for c in range(D // COLS):
            acc[:, cols(c)] += (nn(dqd[...], wq[0:192, cols(c)]) + nn(dkd[...], wq[192:384, cols(c)])
                                + nn(dvd[...], wq[384:576, cols(c)]))
    local_attn_back(0, wqkv_ref.at[1], wout_ref.at[1])
    others(local_attn_back)
    work(7.0)
    ready()
    dx, gg, bg = norm_back(acc[...], xs[...], g_of(1, 0))
    vec_add(1, 0, gg, bg)
    g = carry[...] + dx
    carry[...] = g
    ag_send(g.astype(BF16).astype(F32))

    def mlp_grads(l, glow, then):
        yield now[0], 1.5
        weight_grad_wide(act.at[l], glow, gmat.at[2 * l + 1])
        yield now[0], 1.5
        weight_grad_wide(n2.at[l], du.at[l], gmat.at[2 * l])
        sums["mlp", l] = begin(all_sum(gmat.at[2 * l:2 * l + 2], mlp_out.at[:, l], 2, core_m.at[l], half_m.at[l], full_m.at[l], sub_m.at[l],
                                       (sm_s.at[l], sm_r.at[l]), keep_s.at[3 + l]))

    def att_grads(l):
        for i, t in enumerate((dq, dk, dv)):
            weight_grad(t.at[l], n1.at[l], gatt.at[l, 0], 192 * i)
        weight_grad(o.at[l], low.at[l], gatt.at[l, 0], 576)
        work(1.5)
        sums["att", l] = begin(all_sum(gatt.at[l], att_out.at[l], 1, core_a.at[l], half_a.at[l], full_a.at[l], sub_a.at[l],
                                       (sa_s.at[l], sa_r.at[l]), keep_s.at[9 + l]))

    def layer1_grads():
        yield from after("n2")

        def both(b, r, n):
            n2[1, r] = n
            mlp_both(n, cot_ref[r], wup_ref.at[1], wdown_ref.at[1], act.at[1, r], du.at[1, r])
        yield from taken(n2_all, both, 2.0)
        yield from mlp_grads(1, cot_ref, None)
        yield from after("n1")
        yield from taken(n1_all, lambda b, r, n: qkv_attn(1, b, r, n), 2.0)
        yield from after("dha")
        yield from taken(da_all, lambda b, r, n: qkv_attn_back(1, b, r, n), 1.7)
        yield now[0], 1.5
        att_grads(1)
    grads1 = begin(layer1_grads())

    def back_block(b, r):
        gl = ag[r].astype(BF16)
        gmlow[r] = gl
        mlp_back(r, gl)
    ag_take(back_block, 0.8)
    rs_send(lambda r, c: nt(du[0, r], wup_ref[0, cols(c), :]), 0.7)
    sums["dha"] = begin(gather_x(2, da_all))
    grads0 = begin(mlp_grads(0, gmlow, None))
    dx, gg, bg = norm_back(rs_done(), hs[0], g_of(0, 1))
    vec_add(0, 1, gg, bg)
    dh = carry[...] + dx
    carry[...] = dh
    ag_send(dh.astype(BF16).astype(F32))
    ag_take(lambda b, r: qkv_attn_back(0, b, r, ag[r].astype(BF16)), 1.5)
    att_grads(0)
    rs_send(lambda r, c: nn(dq[0, r], wqkv_ref[0, 0:192, cols(c)]) + nn(dk[0, r], wqkv_ref[0, 192:384, cols(c)])
            + nn(dv[0, r], wqkv_ref[0, 384:576, cols(c)]), 0.7)
    dx, gg, bg = norm_back(rs_done(), x0(me, mine), g_of(0, 0))
    vec_add(0, 0, gg, bg)
    ag_send(carry[...] + dx)
    begin(sum_vecs())
    begin(gather_x(3, lo_out))

    def grad_block(b, r):
        g = ag[r]
        for i in range(2):
            total = jnp.sum(g[SEQ_LEN * i:SEQ_LEN * (i + 1)], axis=0, keepdims=True)
            own = total[:, 0:192]
            for t in range(1, 4):
                own = jnp.where(me == t, total[:, 192 * t:192 * (t + 1)], own)
            sums_all[z, y, core, pl.ds(2 * b + i, 1), 0:192] = own
    ag_take(grad_block, 0.3)
    spreading = begin(spread(sums_all, (st_s, st_r)))
    tg_copy = pltpu.make_async_copy(ag, tg_out, out_s.at[4])
    tg_copy.start()
    finish(spreading)
    tg_copy.wait()
    table_sums()
    work(1.0)
    while running:
        advance(min(running, key=lambda e: e[1]))


def on_device(nz, ny, nx, tokens, cotangent, buckets, time_table, w_qkv, w_out, w_up, w_down, norm_gain, norm_bias):
    trow = jnp.take(time_table, buckets, axis=0).astype(F32).reshape(-1, 1, D)
    ids = jnp.broadcast_to(buckets[:, None], (buckets.shape[0], BLK))
    wqkv = w_qkv.transpose(0, 2, 3, 1).reshape(2, -1, D)
    vm = pl.BlockSpec(memory_space=pltpu.VMEM)
    hbm = pl.BlockSpec(memory_space=pl.ANY)
    sd = jax.ShapeDtypeStruct
    sem = pltpu.SemaphoreType.DMA

    def sum_bufs(n):
        return [
            pltpu.VMEM((2, 2, n, 96, 384), F32),
            pltpu.VMEM((2, 2, n, 192, 384), F32),
            pltpu.VMEM((2, 3, n, 48, 384), F32),
        ]

    def sems(*n):
        return [sem(n), sem(n)]

    lo, tg, table, gain, bias, att, mlp = pl.pallas_call(
        functools.partial(body, nz, ny, nx),
        out_shape=(sd((ROWS, D), F32), sd((ROWS, D), F32), sd((192, 2048), F32), sd((2, 2, D), F32), sd((2, 2, D), F32),
                   sd((2, 1, D, D), F32), sd((2, 2, D, D), F32),
                   sd((3, 3, D, D), F32), sd((2, 2, D, 384), F32), sd((2, 1, D, 384), F32),
                   sd((ROWS, D), F32), sd((ROWS, D), F32), sd((ROWS, D), F32)),
        in_specs=[vm] * 10,
        out_specs=(hbm, hbm, hbm, vm, vm) + (hbm,) * 8,
        scratch_shapes=[
            pltpu.VMEM((4, D, D), F32),
            pltpu.VMEM((2, 1, D, D), F32),
            pltpu.VMEM((8, D), F32),
            pltpu.VMEM((ROWS, D), F32),
            pltpu.VMEM((4, BLK, D), F32),
            pltpu.VMEM((2, HALF, D), F32),
            pltpu.VMEM((2, BLK, D), F32),
            pltpu.VMEM((2, ROWS, D), BF16),
            pltpu.VMEM((2, ROWS, D), BF16),
            pltpu.VMEM((2, ROWS, D), BF16),
            pltpu.VMEM((2, ROWS, 192), BF16),
            pltpu.VMEM((2, ROWS, 192), BF16),
            pltpu.VMEM((2, ROWS, 192), BF16),
            pltpu.VMEM((2, ROWS, 192), BF16),
            pltpu.VMEM((ROWS, D), F32),
            pltpu.VMEM((2, 12, BLK, BLK), F32),
            pltpu.VMEM((2, BLK, D), F32),
            pltpu.VMEM((BLK, D), F32),
            pltpu.VMEM((BLK, D), F32),
            pltpu.VMEM((ROWS, D), BF16),
            pltpu.VMEM((2, ROWS, D), BF16),
            pltpu.VMEM((2, ROWS, D), BF16),
            pltpu.VMEM((2, ROWS, 192), BF16),
            pltpu.VMEM((2, ROWS, 192), BF16),
            pltpu.VMEM((2, ROWS, 192), BF16),
            pltpu.VMEM((3, D, D), BF16),
            pltpu.VMEM((2, D, D), BF16),
            pltpu.VMEM((BLK, D), F32),
            pltpu.VMEM((BLK, D), F32),
            pltpu.VMEM((4, BLK, D), F32),
            pltpu.VMEM((2, BLK, D), F32),
            pltpu.VMEM((3, 1, 48, 384), F32),
            pltpu.VMEM((3, 3, 48, 384), F32),
            pltpu.VMEM((2, 192, 384), F32),
        ] + sum_bufs(2) + sum_bufs(1) + [
            pltpu.VMEM((4, 4, 8, D), F32),
            pltpu.VMEM((4, 4, 2, 8, BLK), F32),
            pltpu.VMEM((4, 4, 2, 8, 256), F32),
        ] + sems(6) + sems(6) + sems(4, 6) + sems(2, 20) + sems(2, 20) + sems(3, 13) + sems(10) + sems(7) + sems(7)
        + [sem((11,)), sem((2,)), sem((2,)), sem((2,)), sem((5,))],
        compiler_params=pltpu.CompilerParams(collective_id=0, has_side_effects=True, vmem_limit_bytes=int(63 * 2 ** 20)),
        name="layers",
    )(tokens, trow, cotangent, ids, wqkv, w_out, w_up, w_down, norm_gain, norm_bias)[:7]
    qkv = att[:, 0, 0:576].reshape(2, 3, 192, D).transpose(0, 3, 1, 2)
    return (lo.astype(BF16), tg, table[:, 0:time_table.shape[0]].T, qkv, att[:, 0, 576:768], mlp[0], mlp[1], gain, bias)


def solution(mesh):
    placed = (
        P("dp", None), P("dp", None), P("dp"), P(), P(None, None, None, "tensor"), P(None, "tensor", None),
        P(None, None, "tensor"), P(None, "tensor", None), P(), P(),
    )
    return jax.shard_map(
        functools.partial(on_device, 4, 4, 4),
        mesh=mesh,
        in_specs=placed,
        out_specs=(
            P("dp", None), P("dp", None), P(None, "tensor"), P(None, None, None, "tensor"), P(None, "tensor", None),
            P(None, None, "tensor"), P(None, "tensor", None), P(), P(),
        ),
        check_vma=False,
    )
```

```python
import functools

import jax
import jax.numpy as jnp
from jax import lax
from jax.experimental import pallas as pl
from jax.experimental.pallas import tpu as pltpu
from jax.sharding import PartitionSpec as P

MESH = pl.DeviceIdType.MESH
F32 = jnp.float32
BF16 = jnp.bfloat16
HEAD_DIM = 64
SEQ_LEN = 64
D = 768
ROWS = 512
BLK = 128
HALF = 64
COLS = 256
EPS = 1e-05
GELU_A = 0.7978845608028654
GELU_B = 0.044715


def nn(a, b):
    return lax.dot_general(a, b, (((1,), (0,)), ((), ())), preferred_element_type=F32)


def nt(a, b):
    return lax.dot_general(a, b, (((1,), (1,)), ((), ())), preferred_element_type=F32)


def tn(a, b):
    return lax.dot_general(a, b, (((0,), (0,)), ((), ())), preferred_element_type=F32)


def norm_parts(x):
    c = x - jnp.mean(x, axis=-1, keepdims=True)
    r = lax.rsqrt(jnp.mean(c * c, axis=-1, keepdims=True) + EPS)
    return c * r, r


def norm(x, g, b):
    return norm_parts(x)[0] * g + b


def norm_back(dn, x, g):
    xh, r = norm_parts(x)
    dx = dn * g
    dx = r * (dx - jnp.mean(dx, axis=-1, keepdims=True) - xh * jnp.mean(dx * xh, axis=-1, keepdims=True))
    return dx, jnp.sum(dn * xh, axis=0, keepdims=True), jnp.sum(dn, axis=0, keepdims=True)


def gelu_cdf(u):
    t = jnp.tanh(GELU_A * (u + GELU_B * (u * u * u)))
    return t, 0.5 + 0.5 * t


def gelu(u):
    return u * gelu_cdf(u)[1]


def gelu_slope(u):
    t, cdf = gelu_cdf(u)
    return cdf + u * (0.5 * (1.0 - t * t)) * (GELU_A * (1.0 + 3.0 * GELU_B * (u * u)))


def body(nz, ny, nx,
         tok_ref, trow_ref, cot_in, ids_ref, wqkv_ref, wout_ref, wup_in, wdown_in, gain_ref, bias_ref,
         lo_out, tg_out, table_out, gain_out, bias_out, att_out, mlp_out, land, core_m, core_a, n1_all, n2_all, da_all,
         cot_ref, wup_ref, wdown_ref, gmat, gatt, vec_ref, ag, sbuf, rh, rf, n1, n2, act, q, k, v, o, u, prob, hs, xs, carry, gmlow, low, du, dq, dk, dv,
         watt, wst, acc, acc2, src_x, take_x,
         mine_w, far_w, stage, half_m, full_m, sub_m, half_a, full_a, sub_a, vecs, ids_all, sums_all, sums_x,
         rs_s, rs_r, ag_s, ag_r, gx_s, gx_r, sm_s, sm_r, sa_s, sa_r, sw_s, sw_r, sv_s, sv_r, si_s, si_r, st_s, st_r, sx_s, sx_r,
         keep_s, stage_s, wst_s, take_s, out_s):
    dp = lax.axis_index("dp")
    me = lax.axis_index("tensor")
    core = lax.rem(dp, 2)
    y = lax.rem(dp // 2, ny)
    z = dp // (2 * ny)
    right = (dp, lax.rem(me + 1, nx))
    left = (dp, lax.rem(me + nx - 1, nx))

    def at(zz, yy, cc):
        return ((lax.rem(zz, nz) * ny + lax.rem(yy, ny)) * 2 + lax.rem(cc, 2), me)

    def along(axis, o):
        return at(z, y + o, core) if axis == 0 else at(z + o, y, core)

    twin = at(z, y, core + 1)

    late = [pltpu.make_async_copy(a_, b_, out_s.at[5 + i])
            for i, (a_, b_) in enumerate(((cot_in, cot_ref), (wup_in, wup_ref), (wdown_in, wdown_ref)))]
    for cp in late:
        cp.start()

    bar = pltpu.get_barrier_semaphore()
    peers = [(dp, lax.rem(me + i, nx)) for i in (1, 2, 3)] + [along(a, i) for a in (0, 1) for i in (1, 2, 3)] + [twin]
    for peer in peers:
        pl.semaphore_signal(bar, inc=1, device_id=peer, device_id_type=MESH)
    pl.semaphore_wait(bar, len(peers))

    def rows(b):
        return pl.ds(pl.multiple_of(b * BLK, BLK), BLK)

    def half(b, i):
        return pl.ds(pl.multiple_of(b * BLK + i * HALF, HALF), HALF)

    def turn(rel):
        return lax.rem(me + rel, nx)

    mine = rows(me)

    now = [5.0]
    free = {"core": 0.0, "yz": 0.0, "x": 0.0}
    running = []

    def work(t):
        now[0] += t

    def link(which, t):
        free[which] = max(now[0], free[which]) + t * 1.0
        return free[which] + 2.0

    def advance(entry):
        now[0] = max(now[0], entry[1])
        got = next(entry[0], None)
        if got is None:
            running.remove(entry)
        else:
            entry[1], entry[2] = got if isinstance(got, tuple) else (got, 0.3)

    def begin(gen):
        entry = [gen, 0.0, 0.0]
        running.append(entry)
        advance(entry)
        return entry

    def idle(until, late=0.5):
        while True:
            fit = [e for e in running if max(now[0], e[1]) + e[2] <= until + late]
            if not fit:
                break
            advance(min(fit, key=lambda e: (max(now[0], e[1]), e[2])))
        now[0] = max(now[0], until)

    def ready():
        idle(now[0])

    def finish(entry):
        while entry in running:
            advance(min(running, key=lambda e: e[1]))

    def after(which):
        while which not in sums or sums[which] in running:
            yield max(now[0], sums[which][1] if which in sums else 0.0) + 0.5, 0.0

    def rs_copy(i):
        src, dst, to = [
            (sbuf.at[0, 0:HALF], rh.at[0], right),
            (sbuf.at[0, HALF:BLK], rh.at[1], left),
            (sbuf.at[1, HALF:BLK], rf.at[0, HALF:BLK], right),
            (sbuf.at[2, 0:HALF], rf.at[1, 0:HALF], left),
            (sbuf.at[1, 0:HALF], rf.at[0, 0:HALF], right),
            (sbuf.at[2, HALF:BLK], rf.at[1, HALF:BLK], left),
        ][i]
        return pltpu.make_async_remote_copy(
            src_ref=src, dst_ref=dst, send_sem=rs_s.at[i], recv_sem=rs_r.at[i], device_id=to, device_id_type=MESH)

    rs_end = [0.0]

    def rs_send(part, cost):
        began = 0.0
        for j, rel in enumerate((2, 1, 3, 0)):
            r = rows(turn(rel))
            for c in range(D // COLS):
                sbuf[j, :, c * COLS:(c + 1) * COLS] = part(r, c)
            work(cost)
            if j == 0:
                rs_copy(0).start()
                rs_copy(1).start()
                began = link("x", 12.500000) - 14.500000
            if j == 1:
                rs_copy(2).start()
            if j == 2:
                rs_copy(3).start()
                idle(began + 6.0)
                rs_copy(0).wait_recv()
                sbuf[1, 0:HALF] += rh[0]
                rs_copy(4).start()
                rs_copy(1).wait_recv()
                sbuf[2, HALF:BLK] += rh[1]
                rs_copy(5).start()
                work(0.2)
        rs_end[0] = began + 14.0
        ready()

    def rs_done():
        idle(rs_end[0])
        for i in range(2, 6):
            rs_copy(i).wait_recv()
        total = sbuf[3] + rf[0] + rf[1]
        for i in range(6):
            rs_copy(i).wait_send()
        work(1.0)
        return total

    def ag_copy(i, arriving=False):
        if arriving:
            b, h = [(3, 0), (1, 1), (3, 1), (1, 0), (2, 0), (2, 1)][i]
        else:
            b, h = [(0, 0), (0, 1), (0, 1), (0, 0), (3, 0), (1, 1)][i]
        at = half(turn(b), h)
        return pltpu.make_async_remote_copy(
            src_ref=ag.at[at], dst_ref=ag.at[at], send_sem=ag_s.at[i], recv_sem=ag_r.at[i],
            device_id=[right, left][i % 2], device_id_type=MESH)

    ag_began = [0.0]

    def ag_send(val):
        ag[mine] = val
        for i in range(4):
            ag_copy(i).start()
        ag_began[0] = link("x", 12.500000) - 14.500000

    def ag_take(fn, cost):
        for j, rel in enumerate((0, 3, 1, 2)):
            blk = turn(rel)
            if j == 1:
                idle(ag_began[0] + 5.7)
                ag_copy(0, True).wait_recv()
                ag_copy(4).start()
                ag_copy(1, True).wait_recv()
                ag_copy(5).start()
                idle(ag_began[0] + 9.9)
                ag_copy(2, True).wait_recv()
            if j == 2:
                ag_copy(3, True).wait_recv()
            if j == 3:
                idle(ag_began[0] + 14.0)
                ag_copy(4, True).wait_recv()
                ag_copy(5, True).wait_recv()
            fn(blk, rows(blk))
            work(cost)
            ready()
        for i in range(6):
            ag_copy(i).wait_send()

    def each(fn, cost):
        for b in range(nx):
            fn(b, slice(b * BLK, (b + 1) * BLK))
            work(cost)
            ready()

    def gather_x(w, dst):
        src = src_x.at[w]

        def copy(i, arriving=False):
            if arriving:
                b, h = [(3, 0), (1, 1), (3, 1), (1, 0), (2, 0), (2, 1)][i]
            else:
                b, h = [(0, 0), (0, 1), (0, 1), (0, 0), (3, 0), (1, 1)][i]
            to = dst.at[half(turn(b), h)]
            fr = to if arriving or i > 3 else src.at[h * HALF:(h + 1) * HALF]
            return pltpu.make_async_remote_copy(
                src_ref=fr, dst_ref=to, send_sem=gx_s.at[w, i], recv_sem=gx_r.at[w, i],
                device_id=[right, left][i % 2], device_id_type=MESH)

        for i in range(4):
            copy(i).start()
        keep = pltpu.make_async_copy(src, dst.at[mine], keep_s.at[5 + w])
        keep.start()
        first = link("x", 4.2)
        link("x", 4.2)
        yield first
        copy(0, True).wait_recv()
        copy(4).start()
        copy(1, True).wait_recv()
        copy(5).start()
        yield link("x", 4.2)
        for i in range(2, 6):
            copy(i, True).wait_recv()
        for i in range(6):
            copy(i).wait_send()
        keep.wait()

    def taken(from_ref, fn, cost):
        def fetch(b):
            return pltpu.make_async_copy(from_ref.at[b * BLK:(b + 1) * BLK], take_x.at[b % 2], take_s.at[b % 2])
        fetch(0).start()
        for b in range(4):
            if b < 3:
                fetch(b + 1).start()
            yield now[0], cost
            fetch(b).wait()
            fn(b, slice(b * BLK, (b + 1) * BLK), take_x[b % 2].astype(BF16))
            work(cost)

    def g_of(l, i):
        return gain_ref[l, i:i + 1, :]

    def b_of(l, i):
        return bias_ref[l, i:i + 1, :]

    def x0(b, r):
        x = tok_ref[r].astype(F32)
        s = lax.broadcasted_iota(jnp.int32, (BLK, 1), 0) < SEQ_LEN
        return x + jnp.where(s, trow_ref[2 * b], trow_ref[2 * b + 1])

    iq = lax.broadcasted_iota(jnp.int32, (BLK, BLK), 0) // SEQ_LEN
    ik = lax.broadcasted_iota(jnp.int32, (BLK, BLK), 1) // SEQ_LEN
    same = iq == ik
    lane = lax.broadcasted_iota(jnp.int32, (1, BLK), 1) // HEAD_DIM
    heads = [(slice(0, 128), (lane == 0).astype(F32).astype(BF16)), (slice(0, 128), (lane == 1).astype(F32).astype(BF16)),
             (slice(128, 192), None)]

    def only(x, m):
        return x if m is None else x * m

    def attn_out(qr, kr, vr, o_, pr):
        outs = []
        for i, (c, m) in enumerate(heads):
            s = nt(only(qr[:, c], m), kr[:, c]) * HEAD_DIM ** -0.5
            s = jnp.where(same, s, -1e30)
            e = jnp.exp(s - jnp.max(s, axis=-1, keepdims=True))
            p = e / jnp.sum(e, axis=-1, keepdims=True)
            pr[i] = p
            outs.append(nn(p.astype(BF16), only(vr[:, c], m)))
        o_[:, 0:128] = (outs[0] + outs[1]).astype(BF16)
        o_[:, 128:192] = outs[2].astype(BF16)

    def qkv_attn(l, b, r, n):
        n1[l, r] = n
        for i, t in enumerate((q, k, v)):
            t[l, r, :] = nt(n, wqkv_ref[l, 192 * i:192 * (i + 1), :]).astype(BF16)
        attn_out(q.at[l, r], k.at[l, r], v.at[l, r], o.at[l, r], prob.at[l, pl.ds(3 * b, 3)])

    def qkv_attn_back(l, b, r, dl):
        low[l, r] = dl
        do = nt(dl, wout_ref[l]).astype(BF16)
        attn_back(q.at[l, r], k.at[l, r], v.at[l, r], prob.at[l, pl.ds(3 * b, 3)], do, dq.at[l, r], dk.at[l, r], dv.at[l, r])

    def attn_back(qr, kr, vr, pr, do, dqr, dkr, dvr):
        got = []
        for i, (c, m) in enumerate(heads):
            p = pr[i]
            pb = p.astype(BF16)
            d = only(do[:, c], m)
            dp_ = nt(d, vr[:, c])
            ds = (p * (dp_ - jnp.sum(p * dp_, axis=-1, keepdims=True))).astype(BF16)
            got.append((nn(ds, only(kr[:, c], m)), tn(ds, only(qr[:, c], m)), tn(pb, d)))
        for t, j, s in ((dqr, 0, HEAD_DIM ** -0.5), (dkr, 1, HEAD_DIM ** -0.5), (dvr, 2, 1.0)):
            t[:, 0:128] = ((got[0][j] + got[1][j]) * s).astype(BF16)
            t[:, 128:192] = (got[2][j] * s).astype(BF16)

    def mlp_up(r, n):
        n2[0, r] = n
        for c in range(D // COLS):
            cs = slice(c * COLS, (c + 1) * COLS)
            up = nn(n, wup_ref[0, :, cs])
            u[r, cs] = up
            act[0, r, cs] = gelu(up).astype(BF16)

    def mlp_back(r, gl):
        for c in range(D // COLS):
            cs = slice(c * COLS, (c + 1) * COLS)
            da = nt(gl, wdown_ref[0, cs, :])
            du[0, r, cs] = (da * gelu_slope(u[r, cs])).astype(BF16)

    def mlp_both(n, gl, wu, wd, a_, d_):
        for c in range(D // COLS):
            cs = slice(c * COLS, (c + 1) * COLS)
            up = nn(n, wu[:, cs])
            t, cdf = gelu_cdf(up)
            a_[:, cs] = (up * cdf).astype(BF16)
            slope = cdf + up * (0.5 * (1.0 - t * t)) * (GELU_A * (1.0 + 3.0 * GELU_B * (up * up)))
            d_[:, cs] = (nt(gl, wd[cs, :]) * slope).astype(BF16)

    def weight_grad(a, b, out, at=0):
        for c in range(D // COLS):
            cs = slice(c * COLS, (c + 1) * COLS)
            out[at:at + 192, cs] = tn(a[:, 0:192], b[:, cs])

    def weight_grad_wide(a, b, out):
        def step(i, _):
            at = pl.ds(pl.multiple_of(i * COLS, COLS), COLS)
            for c in range(D // COLS):
                cs = slice(c * COLS, (c + 1) * COLS)
                out[at, cs] = tn(a[:, at], b[:, cs])
            return 0
        lax.fori_loop(0, D // COLS, step, 0)
        work(1.0)

    def cols(c):
        return slice(c * COLS, (c + 1) * COLS)

    def vec_add(l, i, gg, bg):
        vec_ref[2 * l + i:2 * l + i + 1, :] = gg
        vec_ref[4 + 2 * l + i:5 + 2 * l + i, :] = bg

    def remote(src, dst, sems, i, to):
        return pltpu.make_async_remote_copy(
            src_ref=src, dst_ref=dst, send_sem=sems[0].at[i], recv_sem=sems[1].at[i], device_id=to, device_id_type=MESH)

    def shift1(o_):
        return at(z + core * o_, y + (1 - core) * o_, core)

    def shift2(o_):
        return at(z + (1 - core) * o_, y + core * o_, core)

    pos1 = y + core * (z - y)
    pos2 = z + core * (y - z)
    half_cols = pl.ds(pl.multiple_of(core * 384, 128), 384)
    twin_cols = pl.ds(pl.multiple_of((1 - core) * 384, 128), 384)

    def blk(o_, h=0):
        return lax.rem(pos1 + o_, 4) * 192 + h * 96

    def sub(o_):
        return blk(0) + lax.rem(pos2 + o_, 4) * 48

    def part(of, row, count, cs=half_cols):
        return of.at[:, pl.ds(pl.multiple_of(row, 16), count), cs]

    def add_into(mat, n, row, count, srcs, unit=96):
        unit = min(unit, count)

        def step(i, _):
            for kk in range(n):
                to = pl.ds(pl.multiple_of(row + i * unit, 16), unit)
                fr = pl.ds(pl.multiple_of(i * unit, 16), unit)
                val = mat[kk, to, half_cols]
                for src in srcs:
                    val = val + src[kk, fr, :]
                mat[kk, to, half_cols] = val
            return 0
        if count == unit:
            step(0, 0)
        else:
            lax.fori_loop(0, count // unit, step, 0)

    staging = [False]

    def add_core(mat, n, core_b):
        def fetch(i):
            kk, j = i // 4, i % 4
            return pltpu.make_async_copy(core_b.at[kk, pl.ds(192 * j, 192)], stage.at[i % 2], stage_s.at[i % 2])
        while staging[0]:
            yield now[0] + 1.0, 0.0
        staging[0] = True
        for i in range(2):
            fetch(i).start()
        for i in range(4 * n):
            yield now[0] + (0.8 if i == 0 else 0.0), 0.4
            fetch(i).wait()
            kk, j = i // 4, i % 4
            mat[kk, 192 * j:192 * (j + 1), half_cols] += stage[i % 2]
            if i + 2 < 4 * n:
                fetch(i + 2).start()
            work(0.3)
        staging[0] = False

    def hand_out(src, res, n, sems, keep_s, started=None):
        def copy(i):
            if i < 3:
                return remote(src, part(res, sub(0), 48), sems, i, shift2(i + 1))
            if i > 8:
                ref = part(res, blk((0, 1, 3, 2)[i - 9]), 192)
                return remote(ref, ref, sems, i, twin)
            b, h, to = [(0, 0, 1), (0, 1, 3), (0, 1, 1), (0, 0, 3), (3, 0, 1), (1, 1, 3)][i - 3]
            ref = part(res, blk(b, h), 96)
            return remote(ref, ref, sems, i, shift1(to))

        def landing(i):
            if i < 3:
                ref = part(res, sub(3 - i), 48)
            elif i > 8:
                ref = part(res, lax.rem(pos2 + (0, 1, 3, 2)[i - 9], 4) * 192, 192, twin_cols)
            else:
                b, h = [(3, 0), (1, 1), (3, 1), (1, 0), (2, 0), (2, 1)][i - 3]
                ref = part(res, blk(b, h), 96)
            return remote(ref, ref, sems, i, twin)

        for i in range(3):
            copy(i).start()
        keep = pltpu.make_async_copy(src, part(res, sub(0), 48), keep_s)
        keep.start()
        yield link("yz", 1.6 * n)
        keep.wait()
        for i in range(3):
            landing(i).wait_recv()
        for i in range(3, 7):
            copy(i).start()
        copy(9).start()
        if started is not None:
            started()
        arrive = link("yz", 1.6 * n)
        second = link("yz", 1.6 * n)
        yield arrive
        landing(3).wait_recv()
        copy(7).start()
        landing(4).wait_recv()
        copy(8).start()
        arrive = link("yz", 1.6 * n)
        yield second
        landing(5).wait_recv()
        landing(6).wait_recv()
        copy(10).start()
        copy(11).start()
        yield arrive
        landing(7).wait_recv()
        landing(8).wait_recv()
        copy(12).start()
        for i in range(9):
            copy(i).wait_send()
        yield link("core", 0.5 * n)
        for i in range(9, 13):
            landing(i).wait_recv()
        for i in range(9, 13):
            copy(i).wait_send()

    def all_sum(mat, res, n, core_b, half_b, full_b, sub_b, sems, keep_s):
        def copy(i):
            if i < 6:
                src, dst, to = [
                    (part(mat, blk(2, 0), 96), half_b.at[0], 1),
                    (part(mat, blk(2, 1), 96), half_b.at[1], 3),
                    (part(mat, blk(1, 1), 96), full_b.at[0, :, 96:192], 1),
                    (part(mat, blk(3, 0), 96), full_b.at[1, :, 0:96], 3),
                    (part(mat, blk(1, 0), 96), full_b.at[0, :, 0:96], 1),
                    (part(mat, blk(3, 1), 96), full_b.at[1, :, 96:192], 3),
                ][i]
                return remote(src, dst, sems, 13 + i, shift1(to))
            o_ = i - 5
            return remote(part(mat, sub(o_), 48), sub_b.at[o_ - 1], sems, 13 + i, shift2(o_))

        c0 = remote(part(mat, 0, D, twin_cols), core_b, sems, 22, twin)
        c0.start()
        yield link("core", 2.0 * n)
        c0.wait_recv()
        yield from add_core(mat, n, core_b)
        for i in range(4):
            copy(i).start()
        arrive = link("yz", 1.6 * n)
        link("yz", 1.6 * n)
        yield arrive
        copy(0).wait_recv()
        add_into(mat, n, blk(1, 0), 96, [half_b.at[0]])
        copy(4).start()
        copy(1).wait_recv()
        add_into(mat, n, blk(3, 1), 96, [half_b.at[1]])
        copy(5).start()
        work(0.3 * n)
        yield link("yz", 1.6 * n)
        for i in (2, 3, 4, 5):
            copy(i).wait_recv()
        add_into(mat, n, blk(0), 192, [full_b.at[0], full_b.at[1]])
        for i in (6, 7, 8):
            copy(i).start()
        c0.wait_send()
        work(0.5 * n)
        yield link("yz", 1.6 * n)
        for i in (6, 7, 8):
            copy(i).wait_recv()
        add_into(mat, n, sub(0), 48, [sub_b.at[0], sub_b.at[1], sub_b.at[2]])
        for i in range(9):
            copy(i).wait_send()
        work(0.2 * n)
        yield from hand_out(part(mat, sub(0), 48), res, n, sems, keep_s)

    released = [0]

    def fetch_weights(m, fill, use):
        own = mine_w.at[m]
        sems, keep_ = (sw_s.at[m], sw_r.at[m]), keep_s.at[m]
        fill(own)
        sent = [remote(own, far_w.at[m, pl.ds(3 - i, 1)], sems, 12 + i, (dp, lax.rem(me + i, nx))) for i in (1, 2, 3)]
        for cp in sent:
            cp.start()
        yield link("x", 3.2)
        for cp in sent:
            cp.wait_recv()
        while m > released[0]:
            yield now[0] + 1.0, 0.0

        def let_next():
            released[0] = m + 1
        yield from hand_out(far_w.at[m], land.at[m], 3, sems, keep_, let_next)
        for cp in sent:
            cp.wait_send()
        yield from use()

    def spread(buf, sems):
        def group(i):
            if i < 3:
                return buf.at[z, y, core], along(1, i + 1), lambda: buf.at[lax.rem(z + 3 - i, 4), y, core]
            if i < 6:
                return buf.at[:, y, core], along(0, i - 2), lambda: buf.at[:, lax.rem(y + 6 - i, 4), core]
            return buf.at[:, :, core], twin, lambda: buf.at[:, :, lax.rem(core + 1, 2)]

        for some in ((0, 1, 2), (3, 4, 5), (6,)):
            for i in some:
                src, to, _ = group(i)
                remote(src, src, sems, i, to).start()
            yield now[0] + 5.0
            for i in some:
                src, to, where = group(i)
                remote(where(), where(), sems, i, to).wait_recv()
            for i in some:
                src, to, _ = group(i)
                remote(src, src, sems, i, to).wait_send()

    def spread_sums(g):
        sums_x[me] = jnp.zeros((8, D), F32)
        for i in range(2):
            sums_x[me, i:i + 1, :] = jnp.sum(g[SEQ_LEN * i:SEQ_LEN * (i + 1)], axis=0, keepdims=True)
        sent = [remote(sums_x.at[me], sums_x.at[me], (sx_s, sx_r), i - 1, (dp, lax.rem(me + i, nx))) for i in (1, 2, 3)]
        for cp in sent:
            cp.start()
        yield now[0] + 4.0
        for i in (1, 2, 3):
            ref = sums_x.at[lax.rem(me + 4 - i, nx)]
            remote(ref, ref, (sx_s, sx_r), i - 1, twin).wait_recv()
        for cp in sent:
            cp.wait_send()
        for b in range(4):
            both = sums_x[b, 0:2, :]
            own = both[:, 0:192]
            for t in range(1, 4):
                own = jnp.where(me == t, both[:, 192 * t:192 * (t + 1)], own)
            sums_all[z, y, core, 2 * b:2 * b + 2, 0:192] = own
        yield from spread(sums_all, (st_s, st_r))

    def sum_vecs():
        val = vec_ref[...]
        i = 0
        for stage, (pos, peers_) in enumerate((
                (me, [(dp, lax.rem(me + i_, nx)) for i_ in (1, 2, 3)]),
                (z, [along(1, i_) for i_ in (1, 2, 3)]),
                (y, [along(0, i_) for i_ in (1, 2, 3)]),
                (core, [twin]))):
            count = len(peers_) + 1
            buf = vecs.at[stage]
            buf[pos] = val
            sent = []
            for j, to in enumerate(peers_):
                cp = remote(buf.at[pos], buf.at[pos], (sv_s, sv_r), i + j, to)
                cp.start()
                sent.append(cp)
            yield now[0] + 4.0
            for j in range(len(peers_)):
                ref = buf.at[lax.rem(pos + count - 1 - j, count)]
                remote(ref, ref, (sv_s, sv_r), i + j, twin).wait_recv()
            for cp in sent:
                cp.wait_send()
            i += len(peers_)
            val = buf[0]
            for j in range(1, count):
                val = val + buf[j]
        for l in range(2):
            for w in range(2):
                gain_out[l, w:w + 1, :] = val[2 * l + w:2 * l + w + 1, :]
                bias_out[l, w:w + 1, :] = val[4 + 2 * l + w:5 + 2 * l + w, :]

    def table_sums():
        ids = ids_all[...].reshape(256, BLK)[:, 0:1]
        rest = sums_all[...].reshape(256, 256)[:, 0:192]
        parts = []
        for _ in range(3):
            top = rest.astype(BF16)
            parts.append(top)
            rest = rest - top.astype(F32)
        out = []
        for i in range(4):
            hot = lax.broadcasted_iota(jnp.int32, (256, 512), 1).astype(F32) + float(512 * i) == ids
            hot = hot.astype(F32).astype(BF16)
            to = ag.at[0:192, 0:512] if i % 2 == 0 else ag.at[192:384, 0:512]
            if i > 1:
                out[i - 2].wait()
            to[...] = tn(parts[0], hot) + (tn(parts[1], hot) + tn(parts[2], hot))
            cp = pltpu.make_async_copy(to, table_out.at[:, 512 * i:512 * (i + 1)], out_s.at[i])
            cp.start()
            out.append(cp)
        out[2].wait()
        out[3].wait()

    sums = {}

    for i in range(8):
        ids_all[z, y, core, i:i + 1, :] = jnp.full((1, BLK), ids_ref[i]).astype(F32)
    begin(spread(ids_all, (si_s, si_r)))
    w_row = pl.multiple_of(sub(0), 16)

    def fill_att(ref):
        @pl.when(w_row < 576)
        def _():
            ref[0] = wqkv_ref[1, pl.ds(w_row, 48), half_cols].astype(F32)

        @pl.when(w_row >= 576)
        def _():
            ref[0] = wout_ref[1, pl.ds(w_row - 576, 48), half_cols].astype(F32)

    def fill_up(ref):
        ref[0] = wup_ref[1, pl.ds(w_row, 48), half_cols].astype(F32)

    def fill_down(ref):
        ref[0] = wdown_ref[1, pl.ds(w_row, 48), half_cols].astype(F32)

    def use_att():
        def fetch(i):
            j, h = i // 2, i % 2
            return pltpu.make_async_copy(land.at[0, j, pl.ds(384 * h, 384)], gmat.at[i % 4, 0:384], wst_s.at[i % 4])
        for i in range(4):
            fetch(i).start()
        yield now[0] + 1.5, 0.6
        for i in range(6):
            fetch(i).wait()
            j, h = i // 2, i % 2
            watt[j, 384 * h:384 * (h + 1)] = gmat[i % 4, 0:384].astype(BF16)
            if i < 2:
                fetch(i + 4).start()
            work(0.5)
            if i < 5:
                yield now[0], 0.5

    def nothing():
        yield from ()

    att_weights = begin(fetch_weights(0, fill_att, use_att))
    for cp in late:
        cp.wait()
    up_weights = begin(fetch_weights(1, fill_up, nothing))
    down_weights = begin(fetch_weights(2, fill_down, nothing))

    def first(b, r):
        qkv_attn(0, b, r, norm(x0(b, r), g_of(0, 0), b_of(0, 0)).astype(BF16))
    each(first, 2.4)
    rs_send(lambda r, c: nn(o[0, r], wout_ref[0, :, cols(c)]), 0.2)
    h = rs_done() + x0(me, mine)
    hs[0] = h
    ag_send(norm(h, g_of(0, 1), b_of(0, 1)).astype(BF16).astype(F32))

    def up_block(b, r):
        mlp_up(r, ag[r].astype(BF16))
    ag_take(up_block, 0.5)
    rs_send(lambda r, c: nn(act[0, r], wdown_ref[0, :, cols(c)]), 0.3)
    x1 = rs_done() + hs[0]
    xs[...] = x1

    n1d, lowd, ad, dud = (t.at[1, 0:BLK] for t in (n1, low, act, du))
    dqd, dkd, dvd = (t.at[1, 0:BLK] for t in (dq, dk, dv))

    def shard(t, j):
        return t.at[1, rows(j)]

    def shard_prob(j):
        return prob.at[1, pl.ds(3 * j, 3)]

    n = norm(x1, g_of(1, 0), b_of(1, 0)).astype(BF16)
    n1d[...] = n
    src_x[0] = n.astype(F32)
    sums["n1"] = begin(gather_x(0, n1_all))
    finish(att_weights)

    def local_attn(j, wq, wo):
        for i, t in enumerate((q, k, v)):
            shard(t, j)[...] = nt(n1d[...], wq[192 * i:192 * (i + 1), :]).astype(BF16)
        attn_out(shard(q, j), shard(k, j), shard(v, j), shard(o, j), shard_prob(j))
        for c in range(D // COLS):
            acc[:, cols(c)] += nn(shard(o, j)[...], wo[:, cols(c)])

    def others(fn):
        def step(j, _):
            fn(j + 1, watt.at[j, 0:576], watt.at[j, 576:768])
            return 0
        lax.fori_loop(0, nx - 1, step, 0)

    acc[...] = x1
    local_attn(0, wqkv_ref.at[1], wout_ref.at[1])
    others(local_attn)
    work(4.0)
    ready()
    h = acc[...]
    hs[1] = h
    n = norm(h, g_of(1, 1), b_of(1, 1)).astype(BF16)
    lowd[...] = n
    src_x[1] = n.astype(F32)
    sums["n2"] = begin(gather_x(1, n2_all))
    finish(up_weights)
    finish(down_weights)

    def fetch_mlp(j, w):
        return pltpu.make_async_copy(land.at[1 + w, j], gmat.at[w], wst_s.at[w])

    acc2[...] = jnp.zeros_like(acc2)
    cot_own = cot_ref[mine]
    for w in range(2):
        fetch_mlp(0, w).start()
    for j in range(nx):
        if j == 0:
            wu, wd = wup_ref.at[1], wdown_ref.at[1]
        else:
            wu, wd = wst.at[0], wst.at[1]
            for w in range(2):
                fetch_mlp(j - 1, w).wait()
                wst[w] = gmat[w].astype(BF16)
                if j < nx - 1:
                    fetch_mlp(j, w).start()
        mlp_both(lowd[...], cot_own, wu, wd, ad, dud)
        for c in range(D // COLS):
            acc[:, cols(c)] += nn(ad[...], wd[:, cols(c)])
            acc2[:, cols(c)] += nt(dud[...], wu[cols(c), :])
        work(1.4)
        ready()
    src_x[3] = acc[...].astype(BF16).astype(F32)
    dx, gg, bg = norm_back(acc2[...], hs[1], g_of(1, 1))
    vec_add(1, 1, gg, bg)
    dh = cot_own.astype(F32) + dx
    carry[...] = dh
    lowd[...] = dh.astype(BF16)
    src_x[2] = lowd[...].astype(F32)
    sums["dha"] = begin(gather_x(2, da_all))
    acc[...] = jnp.zeros_like(acc)

    def local_attn_back(j, wq, wo):
        do = nt(lowd[...], wo[...]).astype(BF16)
        attn_back(shard(q, j), shard(k, j), shard(v, j), shard_prob(j), do, dqd, dkd, dvd)
        for c in range(D // COLS):
            acc[:, cols(c)] += (nn(dqd[...], wq[0:192, cols(c)]) + nn(dkd[...], wq[192:384, cols(c)])
                                + nn(dvd[...], wq[384:576, cols(c)]))
    local_attn_back(0, wqkv_ref.at[1], wout_ref.at[1])
    others(local_attn_back)
    work(6.0)
    ready()
    dx, gg, bg = norm_back(acc[...], xs[...], g_of(1, 0))
    vec_add(1, 0, gg, bg)
    g = carry[...] + dx
    carry[...] = g
    ag_send(g.astype(BF16).astype(F32))

    def mlp_grads(l, glow, then):
        yield now[0], 1.0
        weight_grad_wide(act.at[l], glow, gmat.at[2 * l + 1])
        yield now[0], 1.0
        weight_grad_wide(n2.at[l], du.at[l], gmat.at[2 * l])
        sums["mlp", l] = begin(all_sum(gmat.at[2 * l:2 * l + 2], mlp_out.at[:, l], 2, core_m.at[l], half_m.at[l], full_m.at[l], sub_m.at[l],
                                       (sm_s.at[l], sm_r.at[l]), keep_s.at[3 + l]))

    def att_grads(l):
        for i, t in enumerate((dq, dk, dv)):
            weight_grad(t.at[l], n1.at[l], gatt.at[l, 0], 192 * i)
        weight_grad(o.at[l], low.at[l], gatt.at[l, 0], 576)
        work(1.5)
        sums["att", l] = begin(all_sum(gatt.at[l], att_out.at[l], 1, core_a.at[l], half_a.at[l], full_a.at[l], sub_a.at[l],
                                       (sa_s.at[l], sa_r.at[l]), keep_s.at[9 + l]))

    def layer1_grads():
        yield from after("n2")

        def both(b, r, n):
            n2[1, r] = n
            mlp_both(n, cot_ref[r], wup_ref.at[1], wdown_ref.at[1], act.at[1, r], du.at[1, r])
        yield from taken(n2_all, both, 0.8)
        yield from mlp_grads(1, cot_ref, None)
        yield from after("n1")
        yield from taken(n1_all, lambda b, r, n: qkv_attn(1, b, r, n), 1.8)
        yield from after("dha")
        yield from taken(da_all, lambda b, r, n: qkv_attn_back(1, b, r, n), 1.5)
        yield now[0], 1.5
        att_grads(1)
    grads1 = begin(layer1_grads())

    def back_block(b, r):
        gl = ag[r].astype(BF16)
        gmlow[r] = gl
        mlp_back(r, gl)
    ag_take(back_block, 0.5)
    rs_send(lambda r, c: nt(du[0, r], wup_ref[0, cols(c), :]), 0.3)
    grads0 = begin(mlp_grads(0, gmlow, None))
    dx, gg, bg = norm_back(rs_done(), hs[0], g_of(0, 1))
    vec_add(0, 1, gg, bg)
    dh = carry[...] + dx
    carry[...] = dh
    ag_send(dh.astype(BF16).astype(F32))
    ag_take(lambda b, r: qkv_attn_back(0, b, r, ag[r].astype(BF16)), 1.5)
    att_grads(0)
    rs_send(lambda r, c: nn(dq[0, r], wqkv_ref[0, 0:192, cols(c)]) + nn(dk[0, r], wqkv_ref[0, 192:384, cols(c)])
            + nn(dv[0, r], wqkv_ref[0, 384:576, cols(c)]), 0.3)
    dx, gg, bg = norm_back(rs_done(), x0(me, mine), g_of(0, 0))
    vec_add(0, 0, gg, bg)
    g = carry[...] + dx
    ag_send(g)
    begin(sum_vecs())
    spreading = begin(spread_sums(g))

    def grad_block(b, r):
        pass
    begin(gather_x(3, lo_out))
    ag_take(grad_block, 0.0)
    tg_copy = pltpu.make_async_copy(ag, tg_out, out_s.at[4])
    tg_copy.start()
    finish(spreading)
    tg_copy.wait()
    table_sums()
    work(1.0)
    while running:
        advance(min(running, key=lambda e: e[1]))


def on_device(nz, ny, nx, tokens, cotangent, buckets, time_table, w_qkv, w_out, w_up, w_down, norm_gain, norm_bias):
    hot = (buckets[:, None] == jnp.arange(time_table.shape[0], dtype=jnp.int32)[None, :]).astype(BF16)
    trow = nn(hot, time_table).reshape(-1, 1, D)
    wqkv = w_qkv.transpose(0, 2, 3, 1).reshape(2, -1, D)
    vm = pl.BlockSpec(memory_space=pltpu.VMEM)
    hbm = pl.BlockSpec(memory_space=pl.ANY)
    sd = jax.ShapeDtypeStruct
    sem = pltpu.SemaphoreType.DMA

    def sum_bufs(n):
        return [
            pltpu.VMEM((2, 2, n, 96, 384), F32),
            pltpu.VMEM((2, 2, n, 192, 384), F32),
            pltpu.VMEM((2, 3, n, 48, 384), F32),
        ]

    def sems(*n):
        return [sem(n), sem(n)]

    lo, tg, table, gain, bias, att, mlp = pl.pallas_call(
        functools.partial(body, nz, ny, nx),
        out_shape=(sd((ROWS, D), F32), sd((ROWS, D), F32), sd((192, 2048), F32), sd((2, 2, D), F32), sd((2, 2, D), F32),
                   sd((2, 1, D, D), F32), sd((2, 2, D, D), F32),
                   sd((3, 3, D, D), F32), sd((2, 2, D, 384), F32), sd((2, 1, D, 384), F32),
                   sd((ROWS, D), F32), sd((ROWS, D), F32), sd((ROWS, D), F32)),
        in_specs=[vm, vm, hbm, pl.BlockSpec(memory_space=pltpu.SMEM), vm, vm, hbm, hbm, vm, vm],
        out_specs=(hbm, hbm, hbm, vm, vm) + (hbm,) * 8,
        scratch_shapes=[
            pltpu.VMEM((ROWS, D), BF16),
            pltpu.VMEM((2, D, D), BF16),
            pltpu.VMEM((2, D, D), BF16),
            pltpu.VMEM((4, D, D), F32),
            pltpu.VMEM((2, 1, D, D), F32),
            pltpu.VMEM((8, D), F32),
            pltpu.VMEM((ROWS, D), F32),
            pltpu.VMEM((4, BLK, D), F32),
            pltpu.VMEM((2, HALF, D), F32),
            pltpu.VMEM((2, BLK, D), F32),
            pltpu.VMEM((2, ROWS, D), BF16),
            pltpu.VMEM((2, ROWS, D), BF16),
            pltpu.VMEM((2, ROWS, D), BF16),
            pltpu.VMEM((2, ROWS, 192), BF16),
            pltpu.VMEM((2, ROWS, 192), BF16),
            pltpu.VMEM((2, ROWS, 192), BF16),
            pltpu.VMEM((2, ROWS, 192), BF16),
            pltpu.VMEM((ROWS, D), F32),
            pltpu.VMEM((2, 12, BLK, BLK), F32),
            pltpu.VMEM((2, BLK, D), F32),
            pltpu.VMEM((BLK, D), F32),
            pltpu.VMEM((BLK, D), F32),
            pltpu.VMEM((ROWS, D), BF16),
            pltpu.VMEM((2, ROWS, D), BF16),
            pltpu.VMEM((2, ROWS, D), BF16),
            pltpu.VMEM((2, ROWS, 192), BF16),
            pltpu.VMEM((2, ROWS, 192), BF16),
            pltpu.VMEM((2, ROWS, 192), BF16),
            pltpu.VMEM((3, D, D), BF16),
            pltpu.VMEM((2, D, D), BF16),
            pltpu.VMEM((BLK, D), F32),
            pltpu.VMEM((BLK, D), F32),
            pltpu.VMEM((4, BLK, D), F32),
            pltpu.VMEM((2, BLK, D), F32),
            pltpu.VMEM((3, 1, 48, 384), F32),
            pltpu.VMEM((3, 3, 48, 384), F32),
            pltpu.VMEM((2, 192, 384), F32),
        ] + sum_bufs(2) + sum_bufs(1) + [
            pltpu.VMEM((4, 4, 8, D), F32),
            pltpu.VMEM((4, 4, 2, 8, BLK), F32),
            pltpu.VMEM((4, 4, 2, 8, 256), F32),
            pltpu.VMEM((4, 8, D), F32),
        ] + sems(6) + sems(6) + sems(4, 6) + sems(2, 23) + sems(2, 23) + sems(3, 16) + sems(10) + sems(7) + sems(7) + sems(3)
        + [sem((11,)), sem((2,)), sem((4,)), sem((2,)), sem((8,))],
        compiler_params=pltpu.CompilerParams(collective_id=0, has_side_effects=True, vmem_limit_bytes=int(63 * 2 ** 20)),
        name="layers",
    )(tokens, trow, cotangent, buckets, wqkv, w_out, w_up, w_down, norm_gain, norm_bias)[:7]
    qkv = att[:, 0, 0:576].reshape(2, 3, 192, D).transpose(0, 3, 1, 2)
    return (lo.astype(BF16), tg, table[:, 0:time_table.shape[0]].T, qkv, att[:, 0, 576:768], mlp[0], mlp[1], gain, bias)


def solution(mesh):
    placed = (
        P("dp", None), P("dp", None), P("dp"), P(), P(None, None, None, "tensor"), P(None, "tensor", None),
        P(None, None, "tensor"), P(None, "tensor", None), P(), P(),
    )
    return jax.shard_map(
        functools.partial(on_device, 4, 4, 4),
        mesh=mesh,
        in_specs=placed,
        out_specs=(
            P("dp", None), P("dp", None), P(None, "tensor"), P(None, None, None, "tensor"), P(None, "tensor", None),
            P(None, None, "tensor"), P(None, "tensor", None), P(), P(),
        ),
        check_vma=False,
    )
```

```python
import functools

import jax
import jax.numpy as jnp
from jax import lax
from jax.experimental import pallas as pl
from jax.experimental.pallas import tpu as pltpu
from jax.sharding import PartitionSpec as P

MESH = pl.DeviceIdType.MESH
F32 = jnp.float32
BF16 = jnp.bfloat16
HEAD_DIM = 64
SEQ_LEN = 64
D = 768
ROWS = 512
BLK = 128
HALF = 64
COLS = 256
EPS = 1e-05
GELU_A = 0.7978845608028654
GELU_B = 0.044715


def nn(a, b):
    return lax.dot_general(a, b, (((1,), (0,)), ((), ())), preferred_element_type=F32)


def nt(a, b):
    return lax.dot_general(a, b, (((1,), (1,)), ((), ())), preferred_element_type=F32)


def tn(a, b):
    return lax.dot_general(a, b, (((0,), (0,)), ((), ())), preferred_element_type=F32)


def norm_parts(x):
    c = x - jnp.mean(x, axis=-1, keepdims=True)
    r = lax.rsqrt(jnp.mean(c * c, axis=-1, keepdims=True) + EPS)
    return c * r, r


def norm(x, g, b):
    return norm_parts(x)[0] * g + b


def norm_back(dn, x, g):
    xh, r = norm_parts(x)
    dx = dn * g
    dx = r * (dx - jnp.mean(dx, axis=-1, keepdims=True) - xh * jnp.mean(dx * xh, axis=-1, keepdims=True))
    return dx, jnp.sum(dn * xh, axis=0, keepdims=True), jnp.sum(dn, axis=0, keepdims=True)


def gelu_cdf(u):
    t = jnp.tanh(GELU_A * (u + GELU_B * (u * u * u)))
    return t, 0.5 + 0.5 * t


def gelu(u):
    return u * gelu_cdf(u)[1]


def gelu_slope(u):
    t, cdf = gelu_cdf(u)
    return cdf + u * (0.5 * (1.0 - t * t)) * (GELU_A * (1.0 + 3.0 * GELU_B * (u * u)))


def body(nz, ny, nx,
         tok_ref, trow_ref, cot_in, ids_ref, wqkv_ref, wout_ref, wup_in, wdown_in, gain_ref, bias_ref,
         lo_out, tg_out, table_out, gain_out, bias_out, att_out, mlp_out, land, core_m, core_a, n1_all, n2_all, da_all,
         cot_ref, wup_ref, wdown_ref, gmat, gatt, vec_ref, ag, sbuf, rh, rf, n1, n2, act, q, k, v, o, u, prob, hs, xs, carry, gmlow, low, du, dq, dk, dv,
         watt, wst, acc, acc2, src_x, take_x,
         mine_w, far_w, stage, half_m, full_m, sub_m, half_a, full_a, sub_a, vecs, ids_all, sums_all, sums_x,
         rs_s, rs_r, ag_s, ag_r, gx_s, gx_r, sm_s, sm_r, sa_s, sa_r, sw_s, sw_r, sv_s, sv_r, si_s, si_r, st_s, st_r, sx_s, sx_r,
         keep_s, stage_s, wst_s, take_s, out_s):
    dp = lax.axis_index("dp")
    me = lax.axis_index("tensor")
    core = lax.rem(dp, 2)
    y = lax.rem(dp // 2, ny)
    z = dp // (2 * ny)
    right = (dp, lax.rem(me + 1, nx))
    left = (dp, lax.rem(me + nx - 1, nx))

    def at(zz, yy, cc):
        return ((lax.rem(zz, nz) * ny + lax.rem(yy, ny)) * 2 + lax.rem(cc, 2), me)

    def along(axis, o):
        return at(z, y + o, core) if axis == 0 else at(z + o, y, core)

    twin = at(z, y, core + 1)

    late = [pltpu.make_async_copy(a_, b_, out_s.at[5 + i])
            for i, (a_, b_) in enumerate(((cot_in, cot_ref), (wup_in, wup_ref), (wdown_in, wdown_ref)))]
    for cp in late:
        cp.start()

    bar = pltpu.get_barrier_semaphore()
    peers = [(dp, lax.rem(me + i, nx)) for i in (1, 2, 3)] + [along(a, i) for a in (0, 1) for i in (1, 2, 3)] + [twin]
    for peer in peers:
        pl.semaphore_signal(bar, inc=1, device_id=peer, device_id_type=MESH)
    pl.semaphore_wait(bar, len(peers))

    def rows(b):
        return pl.ds(pl.multiple_of(b * BLK, BLK), BLK)

    def half(b, i):
        return pl.ds(pl.multiple_of(b * BLK + i * HALF, HALF), HALF)

    def turn(rel):
        return lax.rem(me + rel, nx)

    mine = rows(me)

    now = [5.0]
    free = {"core": 0.0, "yz": 0.0, "x": 0.0}
    running = []

    def work(t):
        now[0] += t

    def link(which, t):
        free[which] = max(now[0], free[which]) + t * 1.0
        return free[which] + 2.0

    def advance(entry):
        now[0] = max(now[0], entry[1])
        got = next(entry[0], None)
        if got is None:
            running.remove(entry)
        else:
            entry[1], entry[2] = got if isinstance(got, tuple) else (got, 0.3)

    def begin(gen):
        entry = [gen, 0.0, 0.0]
        running.append(entry)
        advance(entry)
        return entry

    def idle(until, late=0.5):
        while True:
            fit = [e for e in running if max(now[0], e[1]) + e[2] <= until + late]
            if not fit:
                break
            advance(min(fit, key=lambda e: (max(now[0], e[1]), e[2])))
        now[0] = max(now[0], until)

    def ready():
        idle(now[0])

    def finish(entry):
        while entry in running:
            advance(min(running, key=lambda e: e[1]))

    def after(which):
        while which not in sums or sums[which] in running:
            yield max(now[0], sums[which][1] if which in sums else 0.0) + 0.5, 0.0

    def rs_copy(i):
        src, dst, to = [
            (sbuf.at[0, 0:HALF], rh.at[0], right),
            (sbuf.at[0, HALF:BLK], rh.at[1], left),
            (sbuf.at[1, HALF:BLK], rf.at[0, HALF:BLK], right),
            (sbuf.at[2, 0:HALF], rf.at[1, 0:HALF], left),
            (sbuf.at[1, 0:HALF], rf.at[0, 0:HALF], right),
            (sbuf.at[2, HALF:BLK], rf.at[1, HALF:BLK], left),
        ][i]
        return pltpu.make_async_remote_copy(
            src_ref=src, dst_ref=dst, send_sem=rs_s.at[i], recv_sem=rs_r.at[i], device_id=to, device_id_type=MESH)

    rs_end = [0.0]

    def rs_send(part, cost):
        began = 0.0
        for j, rel in enumerate((2, 1, 3, 0)):
            r = rows(turn(rel))
            for c in range(D // COLS):
                sbuf[j, :, c * COLS:(c + 1) * COLS] = part(r, c)
            work(cost)
            if j == 0:
                rs_copy(0).start()
                rs_copy(1).start()
                began = link("x", 12.500000) - 14.500000
            if j == 1:
                rs_copy(2).start()
            if j == 2:
                rs_copy(3).start()
                idle(began + 6.0)
                rs_copy(0).wait_recv()
                sbuf[1, 0:HALF] += rh[0]
                rs_copy(4).start()
                rs_copy(1).wait_recv()
                sbuf[2, HALF:BLK] += rh[1]
                rs_copy(5).start()
                work(0.2)
        rs_end[0] = began + 14.0
        ready()

    def rs_done():
        idle(rs_end[0])
        for i in range(2, 6):
            rs_copy(i).wait_recv()
        total = sbuf[3] + rf[0] + rf[1]
        for i in range(6):
            rs_copy(i).wait_send()
        work(1.0)
        return total

    def ag_copy(i, arriving=False):
        if arriving:
            b, h = [(3, 0), (1, 1), (3, 1), (1, 0), (2, 0), (2, 1)][i]
        else:
            b, h = [(0, 0), (0, 1), (0, 1), (0, 0), (3, 0), (1, 1)][i]
        at = half(turn(b), h)
        return pltpu.make_async_remote_copy(
            src_ref=ag.at[at], dst_ref=ag.at[at], send_sem=ag_s.at[i], recv_sem=ag_r.at[i],
            device_id=[right, left][i % 2], device_id_type=MESH)

    ag_began = [0.0]

    def ag_send(val):
        ag[mine] = val
        for i in range(4):
            ag_copy(i).start()
        ag_began[0] = link("x", 12.500000) - 14.500000

    def ag_take(fn, cost):
        for j, rel in enumerate((0, 3, 1, 2)):
            blk = turn(rel)
            if j == 1:
                idle(ag_began[0] + 5.7)
                ag_copy(0, True).wait_recv()
                ag_copy(4).start()
                ag_copy(1, True).wait_recv()
                ag_copy(5).start()
                idle(ag_began[0] + 9.9)
                ag_copy(2, True).wait_recv()
            if j == 2:
                ag_copy(3, True).wait_recv()
            if j == 3:
                idle(ag_began[0] + 14.0)
                ag_copy(4, True).wait_recv()
                ag_copy(5, True).wait_recv()
            fn(blk, rows(blk))
            work(cost)
            ready()
        for i in range(6):
            ag_copy(i).wait_send()

    def each(fn, cost):
        for b in range(nx):
            fn(b, slice(b * BLK, (b + 1) * BLK))
            work(cost)
            ready()

    def gather_x(w, dst):
        src = src_x.at[w]

        def copy(i, arriving=False):
            if arriving:
                b, h = [(3, 0), (1, 1), (3, 1), (1, 0), (2, 0), (2, 1)][i]
            else:
                b, h = [(0, 0), (0, 1), (0, 1), (0, 0), (3, 0), (1, 1)][i]
            to = dst.at[half(turn(b), h)]
            fr = to if arriving or i > 3 else src.at[h * HALF:(h + 1) * HALF]
            return pltpu.make_async_remote_copy(
                src_ref=fr, dst_ref=to, send_sem=gx_s.at[w, i], recv_sem=gx_r.at[w, i],
                device_id=[right, left][i % 2], device_id_type=MESH)

        for i in range(4):
            copy(i).start()
        keep = pltpu.make_async_copy(src, dst.at[mine], keep_s.at[5 + w])
        keep.start()
        first = link("x", 4.2)
        link("x", 4.2)
        yield first
        copy(0, True).wait_recv()
        copy(4).start()
        copy(1, True).wait_recv()
        copy(5).start()
        yield link("x", 4.2)
        for i in range(2, 6):
            copy(i, True).wait_recv()
        for i in range(6):
            copy(i).wait_send()
        keep.wait()

    def taken(from_ref, fn, cost):
        def fetch(b):
            return pltpu.make_async_copy(from_ref.at[b * BLK:(b + 1) * BLK], take_x.at[b % 2], take_s.at[b % 2])
        fetch(0).start()
        for b in range(4):
            if b < 3:
                fetch(b + 1).start()
            yield now[0], cost
            fetch(b).wait()
            fn(b, slice(b * BLK, (b + 1) * BLK), take_x[b % 2].astype(BF16))
            work(cost)

    def g_of(l, i):
        return gain_ref[l, i:i + 1, :]

    def b_of(l, i):
        return bias_ref[l, i:i + 1, :]

    def x0(b, r):
        x = tok_ref[r].astype(F32)
        s = lax.broadcasted_iota(jnp.int32, (BLK, 1), 0) < SEQ_LEN
        return x + jnp.where(s, trow_ref[2 * b], trow_ref[2 * b + 1])

    iq = lax.broadcasted_iota(jnp.int32, (BLK, BLK), 0) // SEQ_LEN
    ik = lax.broadcasted_iota(jnp.int32, (BLK, BLK), 1) // SEQ_LEN
    same = iq == ik
    lane = lax.broadcasted_iota(jnp.int32, (1, BLK), 1) // HEAD_DIM
    heads = [(slice(0, 128), (lane == 0).astype(F32).astype(BF16)), (slice(0, 128), (lane == 1).astype(F32).astype(BF16)),
             (slice(128, 192), None)]

    def only(x, m):
        return x if m is None else x * m

    def attn_out(qr, kr, vr, o_, pr):
        outs = []
        for i, (c, m) in enumerate(heads):
            s = nt(only(qr[:, c], m), kr[:, c]) * HEAD_DIM ** -0.5
            s = jnp.where(same, s, -1e30)
            e = jnp.exp(s - jnp.max(s, axis=-1, keepdims=True))
            p = e / jnp.sum(e, axis=-1, keepdims=True)
            pr[i] = p
            outs.append(nn(p.astype(BF16), only(vr[:, c], m)))
        o_[:, 0:128] = (outs[0] + outs[1]).astype(BF16)
        o_[:, 128:192] = outs[2].astype(BF16)

    def qkv_attn(l, b, r, n):
        n1[l, r] = n
        for i, t in enumerate((q, k, v)):
            t[l, r, :] = nt(n, wqkv_ref[l, 192 * i:192 * (i + 1), :]).astype(BF16)
        attn_out(q.at[l, r], k.at[l, r], v.at[l, r], o.at[l, r], prob.at[l, pl.ds(3 * b, 3)])

    def qkv_attn_back(l, b, r, dl):
        low[l, r] = dl
        do = nt(dl, wout_ref[l]).astype(BF16)
        attn_back(q.at[l, r], k.at[l, r], v.at[l, r], prob.at[l, pl.ds(3 * b, 3)], do, dq.at[l, r], dk.at[l, r], dv.at[l, r])

    def attn_back(qr, kr, vr, pr, do, dqr, dkr, dvr):
        got = []
        for i, (c, m) in enumerate(heads):
            p = pr[i]
            pb = p.astype(BF16)
            d = only(do[:, c], m)
            dp_ = nt(d, vr[:, c])
            ds = (p * (dp_ - jnp.sum(p * dp_, axis=-1, keepdims=True))).astype(BF16)
            got.append((nn(ds, only(kr[:, c], m)), tn(ds, only(qr[:, c], m)), tn(pb, d)))
        for t, j, s in ((dqr, 0, HEAD_DIM ** -0.5), (dkr, 1, HEAD_DIM ** -0.5), (dvr, 2, 1.0)):
            t[:, 0:128] = ((got[0][j] + got[1][j]) * s).astype(BF16)
            t[:, 128:192] = (got[2][j] * s).astype(BF16)

    def mlp_up(r, n):
        n2[0, r] = n
        for c in range(D // COLS):
            cs = slice(c * COLS, (c + 1) * COLS)
            up = nn(n, wup_ref[0, :, cs])
            u[r, cs] = up
            act[0, r, cs] = gelu(up).astype(BF16)

    def mlp_back(r, gl):
        for c in range(D // COLS):
            cs = slice(c * COLS, (c + 1) * COLS)
            da = nt(gl, wdown_ref[0, cs, :])
            du[0, r, cs] = (da * gelu_slope(u[r, cs])).astype(BF16)

    def mlp_both(n, gl, wu, wd, a_, d_):
        for c in range(D // COLS):
            cs = slice(c * COLS, (c + 1) * COLS)
            up = nn(n, wu[:, cs])
            t, cdf = gelu_cdf(up)
            a_[:, cs] = (up * cdf).astype(BF16)
            slope = cdf + up * (0.5 * (1.0 - t * t)) * (GELU_A * (1.0 + 3.0 * GELU_B * (up * up)))
            d_[:, cs] = (nt(gl, wd[cs, :]) * slope).astype(BF16)

    def weight_grad(a, b, out, at=0):
        for c in range(D // COLS):
            cs = slice(c * COLS, (c + 1) * COLS)
            out[at:at + 192, cs] = tn(a[:, 0:192], b[:, cs])

    def weight_grad_wide(a, b, out):
        def step(i, _):
            at = pl.ds(pl.multiple_of(i * COLS, COLS), COLS)
            for c in range(D // COLS):
                cs = slice(c * COLS, (c + 1) * COLS)
                out[at, cs] = tn(a[:, at], b[:, cs])
            return 0
        lax.fori_loop(0, D // COLS, step, 0)
        work(1.0)

    def cols(c):
        return slice(c * COLS, (c + 1) * COLS)

    def vec_add(l, i, gg, bg):
        vec_ref[2 * l + i:2 * l + i + 1, :] = gg
        vec_ref[4 + 2 * l + i:5 + 2 * l + i, :] = bg

    def remote(src, dst, sems, i, to):
        return pltpu.make_async_remote_copy(
            src_ref=src, dst_ref=dst, send_sem=sems[0].at[i], recv_sem=sems[1].at[i], device_id=to, device_id_type=MESH)

    def shift1(o_):
        return at(z + core * o_, y + (1 - core) * o_, core)

    def shift2(o_):
        return at(z + (1 - core) * o_, y + core * o_, core)

    pos1 = y + core * (z - y)
    pos2 = z + core * (y - z)
    half_cols = pl.ds(pl.multiple_of(core * 384, 128), 384)
    twin_cols = pl.ds(pl.multiple_of((1 - core) * 384, 128), 384)

    def blk(o_, h=0):
        return lax.rem(pos1 + o_, 4) * 192 + h * 96

    def sub(o_):
        return blk(0) + lax.rem(pos2 + o_, 4) * 48

    def part(of, row, count, cs=half_cols):
        return of.at[:, pl.ds(pl.multiple_of(row, 16), count), cs]

    def add_into(mat, n, row, count, srcs, unit=96):
        unit = min(unit, count)

        def step(i, _):
            for kk in range(n):
                to = pl.ds(pl.multiple_of(row + i * unit, 16), unit)
                fr = pl.ds(pl.multiple_of(i * unit, 16), unit)
                val = mat[kk, to, half_cols]
                for src in srcs:
                    val = val + src[kk, fr, :]
                mat[kk, to, half_cols] = val
            return 0
        if count == unit:
            step(0, 0)
        else:
            lax.fori_loop(0, count // unit, step, 0)

    staging = [False]

    def add_core(mat, n, core_b):
        def fetch(i):
            kk, j = i // 4, i % 4
            return pltpu.make_async_copy(core_b.at[kk, pl.ds(192 * j, 192)], stage.at[i % 2], stage_s.at[i % 2])
        while staging[0]:
            yield now[0] + 1.0, 0.0
        staging[0] = True
        for i in range(2):
            fetch(i).start()
        for i in range(4 * n):
            yield now[0] + (0.8 if i == 0 else 0.0), 0.4
            fetch(i).wait()
            kk, j = i // 4, i % 4
            mat[kk, 192 * j:192 * (j + 1), half_cols] += stage[i % 2]
            if i + 2 < 4 * n:
                fetch(i + 2).start()
            work(0.3)
        staging[0] = False

    def hand_out(src, res, n, sems, keep_s, started=None):
        def copy(i):
            if i < 3:
                return remote(src, part(res, sub(0), 48), sems, i, shift2(i + 1))
            if i > 8:
                ref = part(res, blk((0, 1, 3, 2)[i - 9]), 192)
                return remote(ref, ref, sems, i, twin)
            b, h, to = [(0, 0, 1), (0, 1, 3), (0, 1, 1), (0, 0, 3), (3, 0, 1), (1, 1, 3)][i - 3]
            ref = part(res, blk(b, h), 96)
            return remote(ref, ref, sems, i, shift1(to))

        def landing(i):
            if i < 3:
                ref = part(res, sub(3 - i), 48)
            elif i > 8:
                ref = part(res, lax.rem(pos2 + (0, 1, 3, 2)[i - 9], 4) * 192, 192, twin_cols)
            else:
                b, h = [(3, 0), (1, 1), (3, 1), (1, 0), (2, 0), (2, 1)][i - 3]
                ref = part(res, blk(b, h), 96)
            return remote(ref, ref, sems, i, twin)

        for i in range(3):
            copy(i).start()
        keep = pltpu.make_async_copy(src, part(res, sub(0), 48), keep_s)
        keep.start()
        yield link("yz", 1.6 * n)
        keep.wait()
        for i in range(3):
            landing(i).wait_recv()
        for i in range(3, 7):
            copy(i).start()
        copy(9).start()
        if started is not None:
            started()
        arrive = link("yz", 1.6 * n)
        second = link("yz", 1.6 * n)
        yield arrive
        landing(3).wait_recv()
        copy(7).start()
        landing(4).wait_recv()
        copy(8).start()
        arrive = link("yz", 1.6 * n)
        yield second
        landing(5).wait_recv()
        landing(6).wait_recv()
        copy(10).start()
        copy(11).start()
        yield arrive
        landing(7).wait_recv()
        landing(8).wait_recv()
        copy(12).start()
        for i in range(9):
            copy(i).wait_send()
        yield link("core", 0.5 * n)
        for i in range(9, 13):
            landing(i).wait_recv()
        for i in range(9, 13):
            copy(i).wait_send()

    def all_sum(mat, res, n, core_b, half_b, full_b, sub_b, sems, keep_s):
        def copy(i):
            if i < 6:
                src, dst, to = [
                    (part(mat, blk(2, 0), 96), half_b.at[0], 1),
                    (part(mat, blk(2, 1), 96), half_b.at[1], 3),
                    (part(mat, blk(1, 1), 96), full_b.at[0, :, 96:192], 1),
                    (part(mat, blk(3, 0), 96), full_b.at[1, :, 0:96], 3),
                    (part(mat, blk(1, 0), 96), full_b.at[0, :, 0:96], 1),
                    (part(mat, blk(3, 1), 96), full_b.at[1, :, 96:192], 3),
                ][i]
                return remote(src, dst, sems, 13 + i, shift1(to))
            o_ = i - 5
            return remote(part(mat, sub(o_), 48), sub_b.at[o_ - 1], sems, 13 + i, shift2(o_))

        c0 = remote(part(mat, 0, D, twin_cols), core_b, sems, 22, twin)
        c0.start()
        yield link("core", 2.0 * n)
        c0.wait_recv()
        yield from add_core(mat, n, core_b)
        for i in range(4):
            copy(i).start()
        arrive = link("yz", 1.6 * n)
        link("yz", 1.6 * n)
        yield arrive
        copy(0).wait_recv()
        add_into(mat, n, blk(1, 0), 96, [half_b.at[0]])
        copy(4).start()
        copy(1).wait_recv()
        add_into(mat, n, blk(3, 1), 96, [half_b.at[1]])
        copy(5).start()
        work(0.3 * n)
        yield link("yz", 1.6 * n)
        for i in (2, 3, 4, 5):
            copy(i).wait_recv()
        add_into(mat, n, blk(0), 192, [full_b.at[0], full_b.at[1]])
        for i in (6, 7, 8):
            copy(i).start()
        c0.wait_send()
        work(0.5 * n)
        yield link("yz", 1.6 * n)
        for i in (6, 7, 8):
            copy(i).wait_recv()
        add_into(mat, n, sub(0), 48, [sub_b.at[0], sub_b.at[1], sub_b.at[2]])
        for i in range(9):
            copy(i).wait_send()
        work(0.2 * n)
        yield from hand_out(part(mat, sub(0), 48), res, n, sems, keep_s)

    released = [0]

    def fetch_weights(m, fill, use):
        own = mine_w.at[m]
        sems, keep_ = (sw_s.at[m], sw_r.at[m]), keep_s.at[m]
        fill(own)
        sent = [remote(own, far_w.at[m, pl.ds(3 - i, 1)], sems, 12 + i, (dp, lax.rem(me + i, nx))) for i in (1, 2, 3)]
        for cp in sent:
            cp.start()
        yield link("x", 3.2)
        for cp in sent:
            cp.wait_recv()
        while m > released[0]:
            yield now[0] + 1.0, 0.0

        def let_next():
            released[0] = m + 1
        yield from hand_out(far_w.at[m], land.at[m], 3, sems, keep_, let_next)
        for cp in sent:
            cp.wait_send()
        yield from use()

    def spread(buf, sems):
        def group(i):
            if i < 3:
                return buf.at[z, y, core], along(1, i + 1), lambda: buf.at[lax.rem(z + 3 - i, 4), y, core]
            if i < 6:
                return buf.at[:, y, core], along(0, i - 2), lambda: buf.at[:, lax.rem(y + 6 - i, 4), core]
            return buf.at[:, :, core], twin, lambda: buf.at[:, :, lax.rem(core + 1, 2)]

        for some in ((0, 1, 2), (3, 4, 5), (6,)):
            for i in some:
                src, to, _ = group(i)
                remote(src, src, sems, i, to).start()
            yield now[0] + 5.0
            for i in some:
                src, to, where = group(i)
                remote(where(), where(), sems, i, to).wait_recv()
            for i in some:
                src, to, _ = group(i)
                remote(src, src, sems, i, to).wait_send()

    def spread_sums(g):
        sums_x[me] = jnp.zeros((8, D), F32)
        for i in range(2):
            sums_x[me, i:i + 1, :] = jnp.sum(g[SEQ_LEN * i:SEQ_LEN * (i + 1)], axis=0, keepdims=True)
        sent = [remote(sums_x.at[me], sums_x.at[me], (sx_s, sx_r), i - 1, (dp, lax.rem(me + i, nx))) for i in (1, 2, 3)]
        for cp in sent:
            cp.start()
        yield now[0] + 4.0
        for i in (1, 2, 3):
            ref = sums_x.at[lax.rem(me + 4 - i, nx)]
            remote(ref, ref, (sx_s, sx_r), i - 1, twin).wait_recv()
        for cp in sent:
            cp.wait_send()
        for b in range(4):
            both = sums_x[b, 0:2, :]
            own = both[:, 0:192]
            for t in range(1, 4):
                own = jnp.where(me == t, both[:, 192 * t:192 * (t + 1)], own)
            sums_all[z, y, core, 2 * b:2 * b + 2, 0:192] = own
        yield from spread(sums_all, (st_s, st_r))

    def sum_vecs():
        val = vec_ref[...]
        i = 0
        for stage, (pos, peers_) in enumerate((
                (me, [(dp, lax.rem(me + i_, nx)) for i_ in (1, 2, 3)]),
                (z, [along(1, i_) for i_ in (1, 2, 3)]),
                (y, [along(0, i_) for i_ in (1, 2, 3)]),
                (core, [twin]))):
            count = len(peers_) + 1
            buf = vecs.at[stage]
            buf[pos] = val
            sent = []
            for j, to in enumerate(peers_):
                cp = remote(buf.at[pos], buf.at[pos], (sv_s, sv_r), i + j, to)
                cp.start()
                sent.append(cp)
            yield now[0] + 4.0
            for j in range(len(peers_)):
                ref = buf.at[lax.rem(pos + count - 1 - j, count)]
                remote(ref, ref, (sv_s, sv_r), i + j, twin).wait_recv()
            for cp in sent:
                cp.wait_send()
            i += len(peers_)
            val = buf[0]
            for j in range(1, count):
                val = val + buf[j]
        for l in range(2):
            for w in range(2):
                gain_out[l, w:w + 1, :] = val[2 * l + w:2 * l + w + 1, :]
                bias_out[l, w:w + 1, :] = val[4 + 2 * l + w:5 + 2 * l + w, :]

    def table_sums():
        ids = ids_all[...].reshape(256, BLK)[:, 0:1]
        rest = sums_all[...].reshape(256, 256)[:, 0:192]
        parts = []
        for _ in range(3):
            top = rest.astype(BF16)
            parts.append(top)
            rest = rest - top.astype(F32)
        out = []
        for i in range(4):
            hot = lax.broadcasted_iota(jnp.int32, (256, 512), 1).astype(F32) + float(512 * i) == ids
            hot = hot.astype(F32).astype(BF16)
            to = ag.at[0:192, 0:512] if i % 2 == 0 else ag.at[192:384, 0:512]
            if i > 1:
                out[i - 2].wait()
            to[...] = tn(parts[0], hot) + (tn(parts[1], hot) + tn(parts[2], hot))
            cp = pltpu.make_async_copy(to, table_out.at[:, 512 * i:512 * (i + 1)], out_s.at[i])
            cp.start()
            out.append(cp)
        out[2].wait()
        out[3].wait()

    sums = {}

    for i in range(8):
        ids_all[z, y, core, i:i + 1, :] = jnp.full((1, BLK), ids_ref[i]).astype(F32)
    begin(spread(ids_all, (si_s, si_r)))
    w_row = pl.multiple_of(sub(0), 16)

    def fill_att(ref):
        @pl.when(w_row < 576)
        def _():
            ref[0] = wqkv_ref[1, pl.ds(w_row, 48), half_cols].astype(F32)

        @pl.when(w_row >= 576)
        def _():
            ref[0] = wout_ref[1, pl.ds(w_row - 576, 48), half_cols].astype(F32)

    def fill_up(ref):
        ref[0] = wup_ref[1, pl.ds(w_row, 48), half_cols].astype(F32)

    def fill_down(ref):
        ref[0] = wdown_ref[1, pl.ds(w_row, 48), half_cols].astype(F32)

    def use_att():
        def fetch(i):
            j, h = i // 2, i % 2
            return pltpu.make_async_copy(land.at[0, j, pl.ds(384 * h, 384)], gmat.at[i % 4, 0:384], wst_s.at[i % 4])
        for i in range(4):
            fetch(i).start()
        yield now[0] + 1.5, 0.6
        for i in range(6):
            fetch(i).wait()
            j, h = i // 2, i % 2
            watt[j, 384 * h:384 * (h + 1)] = gmat[i % 4, 0:384].astype(BF16)
            if i < 2:
                fetch(i + 4).start()
            work(0.5)
            if i < 5:
                yield now[0], 0.5

    def nothing():
        yield from ()

    att_weights = begin(fetch_weights(0, fill_att, use_att))
    for cp in late:
        cp.wait()
    up_weights = begin(fetch_weights(1, fill_up, nothing))
    down_weights = begin(fetch_weights(2, fill_down, nothing))

    def first(b, r):
        qkv_attn(0, b, r, norm(x0(b, r), g_of(0, 0), b_of(0, 0)).astype(BF16))
    each(first, 2.4)
    rs_send(lambda r, c: nn(o[0, r], wout_ref[0, :, cols(c)]), 0.2)
    h = rs_done() + x0(me, mine)
    hs[0] = h
    ag_send(norm(h, g_of(0, 1), b_of(0, 1)).astype(BF16).astype(F32))

    def up_block(b, r):
        mlp_up(r, ag[r].astype(BF16))
    ag_take(up_block, 0.5)
    rs_send(lambda r, c: nn(act[0, r], wdown_ref[0, :, cols(c)]), 0.3)
    x1 = rs_done() + hs[0]
    xs[...] = x1

    n1d, lowd, ad, dud = (t.at[1, 0:BLK] for t in (n1, low, act, du))
    dqd, dkd, dvd = (t.at[1, 0:BLK] for t in (dq, dk, dv))

    def shard(t, j):
        return t.at[1, rows(j)]

    def shard_prob(j):
        return prob.at[1, pl.ds(3 * j, 3)]

    n = norm(x1, g_of(1, 0), b_of(1, 0)).astype(BF16)
    n1d[...] = n
    src_x[0] = n.astype(F32)
    sums["n1"] = begin(gather_x(0, n1_all))
    finish(att_weights)

    def local_attn(j, wq, wo):
        for i, t in enumerate((q, k, v)):
            shard(t, j)[...] = nt(n1d[...], wq[192 * i:192 * (i + 1), :]).astype(BF16)
        attn_out(shard(q, j), shard(k, j), shard(v, j), shard(o, j), shard_prob(j))
        for c in range(D // COLS):
            acc[:, cols(c)] += nn(shard(o, j)[...], wo[:, cols(c)])

    def others(fn):
        def step(j, _):
            fn(j + 1, watt.at[j, 0:576], watt.at[j, 576:768])
            return 0
        lax.fori_loop(0, nx - 1, step, 0)

    acc[...] = x1
    local_attn(0, wqkv_ref.at[1], wout_ref.at[1])
    others(local_attn)
    work(4.0)
    ready()
    h = acc[...]
    hs[1] = h
    n = norm(h, g_of(1, 1), b_of(1, 1)).astype(BF16)
    lowd[...] = n
    src_x[1] = n.astype(F32)
    sums["n2"] = begin(gather_x(1, n2_all))
    finish(up_weights)
    finish(down_weights)

    def fetch_mlp(j, w):
        return pltpu.make_async_copy(land.at[1 + w, j], gmat.at[w], wst_s.at[w])

    acc2[...] = jnp.zeros_like(acc2)
    cot_own = cot_ref[mine]
    for w in range(2):
        fetch_mlp(0, w).start()
    for j in range(nx):
        if j == 0:
            wu, wd = wup_ref.at[1], wdown_ref.at[1]
        else:
            wu, wd = wst.at[0], wst.at[1]
            for w in range(2):
                fetch_mlp(j - 1, w).wait()
                wst[w] = gmat[w].astype(BF16)
                if j < nx - 1:
                    fetch_mlp(j, w).start()
        mlp_both(lowd[...], cot_own, wu, wd, ad, dud)
        for c in range(D // COLS):
            acc[:, cols(c)] += nn(ad[...], wd[:, cols(c)])
            acc2[:, cols(c)] += nt(dud[...], wu[cols(c), :])
        work(1.4)
        ready()
    src_x[3] = acc[...].astype(BF16).astype(F32)
    dx, gg, bg = norm_back(acc2[...], hs[1], g_of(1, 1))
    vec_add(1, 1, gg, bg)
    dh = cot_own.astype(F32) + dx
    carry[...] = dh
    lowd[...] = dh.astype(BF16)
    src_x[2] = lowd[...].astype(F32)
    acc[...] = jnp.zeros_like(acc)

    def local_attn_back(j, wq, wo):
        do = nt(lowd[...], wo[...]).astype(BF16)
        attn_back(shard(q, j), shard(k, j), shard(v, j), shard_prob(j), do, dqd, dkd, dvd)
        for c in range(D // COLS):
            acc[:, cols(c)] += (nn(dqd[...], wq[0:192, cols(c)]) + nn(dkd[...], wq[192:384, cols(c)])
                                + nn(dvd[...], wq[384:576, cols(c)]))
    local_attn_back(0, wqkv_ref.at[1], wout_ref.at[1])
    others(local_attn_back)
    work(6.0)
    ready()
    dx, gg, bg = norm_back(acc[...], xs[...], g_of(1, 0))
    vec_add(1, 0, gg, bg)
    g = carry[...] + dx
    carry[...] = g
    ag_send(g.astype(BF16).astype(F32))

    def mlp_grads(l, glow, then):
        yield now[0], 1.0
        weight_grad_wide(act.at[l], glow, gmat.at[2 * l + 1])
        yield now[0], 1.0
        weight_grad_wide(n2.at[l], du.at[l], gmat.at[2 * l])
        sums["mlp", l] = begin(all_sum(gmat.at[2 * l:2 * l + 2], mlp_out.at[:, l], 2, core_m.at[l], half_m.at[l], full_m.at[l], sub_m.at[l],
                                       (sm_s.at[l], sm_r.at[l]), keep_s.at[3 + l]))

    def att_grads(l):
        for i, t in enumerate((dq, dk, dv)):
            weight_grad(t.at[l], n1.at[l], gatt.at[l, 0], 192 * i)
        weight_grad(o.at[l], low.at[l], gatt.at[l, 0], 576)
        work(1.5)
        sums["att", l] = begin(all_sum(gatt.at[l], att_out.at[l], 1, core_a.at[l], half_a.at[l], full_a.at[l], sub_a.at[l],
                                       (sa_s.at[l], sa_r.at[l]), keep_s.at[9 + l]))

    def layer1_grads():
        yield from after("n2")

        def both(b, r, n):
            n2[1, r] = n
            mlp_both(n, cot_ref[r], wup_ref.at[1], wdown_ref.at[1], act.at[1, r], du.at[1, r])
        yield from taken(n2_all, both, 0.8)
        yield from mlp_grads(1, cot_ref, None)
        yield from after("n1")
        yield from taken(n1_all, lambda b, r, n: qkv_attn(1, b, r, n), 1.8)
        yield from after("dha")
        yield from taken(da_all, lambda b, r, n: qkv_attn_back(1, b, r, n), 1.5)
        yield now[0], 1.5
        att_grads(1)
    grads1 = begin(layer1_grads())

    def back_block(b, r):
        gl = ag[r].astype(BF16)
        gmlow[r] = gl
        mlp_back(r, gl)
    ag_take(back_block, 0.5)
    rs_send(lambda r, c: nt(du[0, r], wup_ref[0, cols(c), :]), 0.3)
    sums["dha"] = begin(gather_x(2, da_all))
    grads0 = begin(mlp_grads(0, gmlow, None))
    dx, gg, bg = norm_back(rs_done(), hs[0], g_of(0, 1))
    vec_add(0, 1, gg, bg)
    dh = carry[...] + dx
    carry[...] = dh
    ag_send(dh.astype(BF16).astype(F32))
    ag_take(lambda b, r: qkv_attn_back(0, b, r, ag[r].astype(BF16)), 1.5)
    att_grads(0)
    rs_send(lambda r, c: nn(dq[0, r], wqkv_ref[0, 0:192, cols(c)]) + nn(dk[0, r], wqkv_ref[0, 192:384, cols(c)])
            + nn(dv[0, r], wqkv_ref[0, 384:576, cols(c)]), 0.3)
    dx, gg, bg = norm_back(rs_done(), x0(me, mine), g_of(0, 0))
    vec_add(0, 0, gg, bg)
    g = carry[...] + dx
    ag_send(g)
    begin(sum_vecs())
    spreading = begin(spread_sums(g))

    def grad_block(b, r):
        pass
    begin(gather_x(3, lo_out))
    ag_take(grad_block, 0.0)
    tg_copy = pltpu.make_async_copy(ag, tg_out, out_s.at[4])
    tg_copy.start()
    finish(spreading)
    tg_copy.wait()
    table_sums()
    work(1.0)
    while running:
        advance(min(running, key=lambda e: e[1]))


def on_device(nz, ny, nx, tokens, cotangent, buckets, time_table, w_qkv, w_out, w_up, w_down, norm_gain, norm_bias):
    hot = (buckets[:, None] == jnp.arange(time_table.shape[0], dtype=jnp.int32)[None, :]).astype(BF16)
    trow = nn(hot, time_table).reshape(-1, 1, D)
    wqkv = w_qkv.transpose(0, 2, 3, 1).reshape(2, -1, D)
    vm = pl.BlockSpec(memory_space=pltpu.VMEM)
    hbm = pl.BlockSpec(memory_space=pl.ANY)
    sd = jax.ShapeDtypeStruct
    sem = pltpu.SemaphoreType.DMA

    def sum_bufs(n):
        return [
            pltpu.VMEM((2, 2, n, 96, 384), F32),
            pltpu.VMEM((2, 2, n, 192, 384), F32),
            pltpu.VMEM((2, 3, n, 48, 384), F32),
        ]

    def sems(*n):
        return [sem(n), sem(n)]

    lo, tg, table, gain, bias, att, mlp = pl.pallas_call(
        functools.partial(body, nz, ny, nx),
        out_shape=(sd((ROWS, D), F32), sd((ROWS, D), F32), sd((192, 2048), F32), sd((2, 2, D), F32), sd((2, 2, D), F32),
                   sd((2, 1, D, D), F32), sd((2, 2, D, D), F32),
                   sd((3, 3, D, D), F32), sd((2, 2, D, 384), F32), sd((2, 1, D, 384), F32),
                   sd((ROWS, D), F32), sd((ROWS, D), F32), sd((ROWS, D), F32)),
        in_specs=[vm, vm, hbm, pl.BlockSpec(memory_space=pltpu.SMEM), vm, vm, hbm, hbm, vm, vm],
        out_specs=(hbm, hbm, hbm, vm, vm) + (hbm,) * 8,
        scratch_shapes=[
            pltpu.VMEM((ROWS, D), BF16),
            pltpu.VMEM((2, D, D), BF16),
            pltpu.VMEM((2, D, D), BF16),
            pltpu.VMEM((4, D, D), F32),
            pltpu.VMEM((2, 1, D, D), F32),
            pltpu.VMEM((8, D), F32),
            pltpu.VMEM((ROWS, D), F32),
            pltpu.VMEM((4, BLK, D), F32),
            pltpu.VMEM((2, HALF, D), F32),
            pltpu.VMEM((2, BLK, D), F32),
            pltpu.VMEM((2, ROWS, D), BF16),
            pltpu.VMEM((2, ROWS, D), BF16),
            pltpu.VMEM((2, ROWS, D), BF16),
            pltpu.VMEM((2, ROWS, 192), BF16),
            pltpu.VMEM((2, ROWS, 192), BF16),
            pltpu.VMEM((2, ROWS, 192), BF16),
            pltpu.VMEM((2, ROWS, 192), BF16),
            pltpu.VMEM((ROWS, D), F32),
            pltpu.VMEM((2, 12, BLK, BLK), F32),
            pltpu.VMEM((2, BLK, D), F32),
            pltpu.VMEM((BLK, D), F32),
            pltpu.VMEM((BLK, D), F32),
            pltpu.VMEM((ROWS, D), BF16),
            pltpu.VMEM((2, ROWS, D), BF16),
            pltpu.VMEM((2, ROWS, D), BF16),
            pltpu.VMEM((2, ROWS, 192), BF16),
            pltpu.VMEM((2, ROWS, 192), BF16),
            pltpu.VMEM((2, ROWS, 192), BF16),
            pltpu.VMEM((3, D, D), BF16),
            pltpu.VMEM((2, D, D), BF16),
            pltpu.VMEM((BLK, D), F32),
            pltpu.VMEM((BLK, D), F32),
            pltpu.VMEM((4, BLK, D), F32),
            pltpu.VMEM((2, BLK, D), F32),
            pltpu.VMEM((3, 1, 48, 384), F32),
            pltpu.VMEM((3, 3, 48, 384), F32),
            pltpu.VMEM((2, 192, 384), F32),
        ] + sum_bufs(2) + sum_bufs(1) + [
            pltpu.VMEM((4, 4, 8, D), F32),
            pltpu.VMEM((4, 4, 2, 8, BLK), F32),
            pltpu.VMEM((4, 4, 2, 8, 256), F32),
            pltpu.VMEM((4, 8, D), F32),
        ] + sems(6) + sems(6) + sems(4, 6) + sems(2, 23) + sems(2, 23) + sems(3, 16) + sems(10) + sems(7) + sems(7) + sems(3)
        + [sem((11,)), sem((2,)), sem((4,)), sem((2,)), sem((8,))],
        compiler_params=pltpu.CompilerParams(collective_id=0, has_side_effects=True, vmem_limit_bytes=int(63 * 2 ** 20)),
        name="layers",
    )(tokens, trow, cotangent, buckets, wqkv, w_out, w_up, w_down, norm_gain, norm_bias)[:7]
    qkv = att[:, 0, 0:576].reshape(2, 3, 192, D).transpose(0, 3, 1, 2)
    return (lo.astype(BF16), tg, table[:, 0:time_table.shape[0]].T, qkv, att[:, 0, 576:768], mlp[0], mlp[1], gain, bias)


def solution(mesh):
    placed = (
        P("dp", None), P("dp", None), P("dp"), P(), P(None, None, None, "tensor"), P(None, "tensor", None),
        P(None, None, "tensor"), P(None, "tensor", None), P(), P(),
    )
    return jax.shard_map(
        functools.partial(on_device, 4, 4, 4),
        mesh=mesh,
        in_specs=placed,
        out_specs=(
            P("dp", None), P("dp", None), P(None, "tensor"), P(None, None, None, "tensor"), P(None, "tensor", None),
            P(None, None, "tensor"), P(None, "tensor", None), P(), P(),
        ),
        check_vma=False,
    )
```
